128 devices in a mesh: dom: 128 (over y, z, x, core).
Axes of the slice: x: 4, y: 4, z: 4, core: 2. Of those that a mesh axis runs over, the one named last changes fastest.
Arguments:
- features: float32 [524288, 128], P('dom'), may hold values from -6 to 6
- owner: int32 [524288], P('dom'), may hold values from 0 to 127, as said below
- slot: int32 [524288], P('dom'), may hold values from 0 to 4095
- send_blocks: int32 [128, 128, 1], P('dom'), may hold values from 0 to 31
- tile_row: int32 [32768], P('dom'), may hold values from 0 to 31
- tile_col: int32 [32768], P('dom'), may hold values from 0 to 159
- tile_vals: int32 [32768, 128, 128], P('dom'), may hold values 0 or 1
- tile_count: int32 [128], P('dom'), may hold values from 64 to 256, as said below
- w_self1: bfloat16 [128, 256], replicated, may hold values from -0.5 to 0.5
- w_neigh1: bfloat16 [128, 256], replicated, may hold values from -4.21875 to 4.21875
- w_self2: bfloat16 [256, 256], replicated, may hold values from -0.375 to 0.375
- w_neigh2: bfloat16 [256, 256], replicated, may hold values from -3 to 3
Outputs:
- embed: bfloat16 [524288, 256], P('dom')
The draws below stay inside these ranges and needn't reach their ends.
Inputs may be any that keep to these rules, and one draw needn't show every extreme that they name: Each partition's nodes in file order go exactly 4096 // 128 to every partition; the pairs (owner, slot) name every row of every partition once. `tile_count`: some partition uses all its tile slots.
All inputs are finite; a program needn't handle non-finite values. No bound on the sum of `tile_vals` on one device may be relied on, other than what follows from the above.
Results may differ from the reference program's by a relative error of at most 0.0043.
Values may be sent and summed in bfloat16 or wider, within the bound.
No kernel may reach another device: no remote copies, remote signals or barrier semaphores. Data moves between devices by JAX's collectives and lax.ppermute only.
A program may use at most 192 MiB of HBM per device.

```python
import jax
import jax.numpy as jnp
from jax import lax

F = 128
H = 256
BLK = 128
HB = 1
ROWS_DEV = 4096
TILES_DEV = 256
NB = 32
NODES = 524288
TILES = 32768
HALO_SLOTS = 128
N_DOM = 128


def placement_tables(key):
    first = jax.random.permutation(jax.random.fold_in(key, 101), ROWS_DEV)
    second = jax.random.permutation(jax.random.fold_in(key, 102), ROWS_DEV)
    index = jnp.arange(NODES)
    source = index // ROWS_DEV
    local = index % ROWS_DEV
    owners = (source + first[local] % N_DOM) % N_DOM
    return (owners.astype(jnp.int32), second[local].astype(jnp.int32))


def draw_owner(key, part):
    owners, places = placement_tables(key)
    return owners


def draw_slot(key, part):
    owners, places = placement_tables(key)
    return places


def draw_tile_col(key, part):
    key = jax.random.fold_in(key, 7)
    pick = jax.random.randint(jax.random.fold_in(key, 1), (TILES,), 0, 8)
    local = jax.random.randint(jax.random.fold_in(key, 2), (TILES,), 0, NB)
    remote = NB + jax.random.randint(jax.random.fold_in(key, 3), (TILES,), 0, HALO_SLOTS)
    return jnp.where(pick < 5, remote, local).astype(jnp.int32)


def draw_tile_count(key, part):
    key = jax.random.fold_in(key, 11)
    counts = jax.random.randint(jax.random.fold_in(key, 1), (N_DOM,), TILES_DEV // 4, TILES_DEV + 1)
    fullest = jax.random.randint(jax.random.fold_in(key, 2), (), 0, N_DOM)
    return jnp.where(jnp.arange(N_DOM) == fullest, TILES_DEV, counts).astype(jnp.int32)


def touch_ends(array, stream_key, least, high):
    longest = array.shape.index(max(array.shape))
    spots = []
    for shift in (0, 1):
        where = [jax.random.randint(jax.random.fold_in(stream_key, axis), (), 0, length) for axis, length in enumerate(array.shape)]
        where[longest] = (where[longest] + shift) % array.shape[longest]
        spots.append(tuple(where))
    return array.at[spots[0]].set(least).at[spots[1]].set(high)


def level_of(key, extent, pieces, smallest, high):
    def one(position, blocks):
        draws = jax.random.uniform(jax.random.fold_in(jax.random.fold_in(key, 6), position), (blocks,), jnp.float32, smallest / len(pieces), high / len(pieces))
        return jnp.repeat(jnp.exp(draws), extent[position] // blocks).reshape((-1,) + (1,) * (len(extent) - position - 1))

    loudness = one(*pieces[0])
    for cut in pieces[1:]:
        loudness = loudness * one(*cut)
    return loudness


def scatter_about(key, extent, deviation, limit, cuts=(), kind=jnp.bfloat16):
    gain = level_of(key, extent, cuts, -0.22, 0.18) if cuts else 1.0
    entries = jax.random.normal(key, extent, jnp.float32) * deviation * gain
    return jnp.minimum(jnp.maximum(entries, -limit), limit).astype(kind)


def setup_inputs(seed: int = 0) -> dict:
    splits = jax.random.split(jax.random.key(seed), 13)
    features = scatter_about(splits[0], (NODES, F), 1.0, 6.0, ((0, 128),), jnp.float32)
    owner = draw_owner(jax.random.fold_in(splits[12], 71), 0)
    slot = draw_slot(jax.random.fold_in(splits[12], 71), 0)
    send_blocks = touch_ends(jax.random.randint(splits[3], (N_DOM, N_DOM, HB), 0, NB), jax.random.fold_in(splits[3], 1), 0, NB - 1).astype(jnp.int32)
    tile_row = touch_ends(jax.random.randint(splits[4], (TILES,), 0, NB), jax.random.fold_in(splits[4], 1), 0, NB - 1).astype(jnp.int32)
    tile_col = draw_tile_col(jax.random.fold_in(splits[12], 71), 0)
    tile_vals = touch_ends((jax.random.randint(splits[6], (TILES, BLK, BLK), 0, 16) < 1).astype(jnp.int32), jax.random.fold_in(splits[6], 1), 0, 1)
    tile_count = draw_tile_count(jax.random.fold_in(splits[12], 71), 0)
    w_self1 = scatter_about(splits[8], (F, H), F ** -0.5, 0.5)
    w_neigh1 = scatter_about(splits[9], (F, H), (8.0 / F ** 0.5), 4.21875)
    w_self2 = scatter_about(splits[10], (H, H), H ** -0.5, 0.375)
    w_neigh2 = scatter_about(splits[11], (H, H), (8.0 / H ** 0.5), 3.0)
    return dict(features=features, owner=owner, slot=slot, send_blocks=send_blocks, tile_row=tile_row, tile_col=tile_col, tile_vals=tile_vals, tile_count=tile_count, w_self1=w_self1, w_neigh1=w_neigh1, w_self2=w_self2, w_neigh2=w_neigh2)


def degrees(tile_row, tile_vals, tile_count):
    valid = (jnp.arange(TILES_DEV)[None, :] < tile_count[:, None]).astype(jnp.float32)
    sums = jnp.sum(tile_vals, axis=2).astype(jnp.float32).reshape(N_DOM, TILES_DEV, BLK) * valid[:, :, None]
    rows = tile_row.reshape(N_DOM, TILES_DEV)

    def place(row_ids, values):
        return jnp.zeros((NB, BLK), jnp.float32).at[row_ids].add(values)

    return jax.vmap(place)(rows, sums), valid


def aggregate(node_rows, send_blocks, tile_row, tile_col, tile_vals, valid, degree):
    width = node_rows.shape[1]
    blocks = node_rows.reshape(N_DOM, NB, BLK, width)
    rows = tile_row.reshape(N_DOM, TILES_DEV)
    cols = tile_col.reshape(N_DOM, TILES_DEV)
    vals = tile_vals.reshape(N_DOM, TILES_DEV, BLK, BLK)

    def one(index):
        picks = lax.dynamic_index_in_dim(send_blocks, index, 1, keepdims=False)
        remote = blocks[jnp.arange(N_DOM)[:, None], picks]
        own = lax.dynamic_index_in_dim(blocks, index, 0, keepdims=False)
        table = jnp.concatenate([own, remote.reshape(HALO_SLOTS, BLK, width)], axis=0)
        chosen = table[lax.dynamic_index_in_dim(cols, index, 0, keepdims=False)].astype(jnp.float32)
        tiles = lax.dynamic_index_in_dim(vals, index, 0, keepdims=False).astype(jnp.float32)
        prod = jnp.einsum("tij,tjw->tiw", tiles, chosen)
        prod = prod * lax.dynamic_index_in_dim(valid, index, 0, keepdims=False)[:, None, None]
        acc = jnp.zeros((NB, BLK, width), jnp.float32).at[lax.dynamic_index_in_dim(rows, index, 0, keepdims=False)].add(prod)
        return acc

    total = lax.map(one, jnp.arange(N_DOM).astype(jnp.int32))
    total = total / jnp.maximum(degree, 1.0)[:, :, :, None]
    return total.reshape(NODES, width)


def reference(features, owner, slot, send_blocks, tile_row, tile_col, tile_vals, tile_count, w_self1, w_neigh1, w_self2, w_neigh2):
    target = owner * ROWS_DEV + slot
    relaid = jnp.zeros((NODES, F), jnp.bfloat16).at[target].set(features.astype(jnp.bfloat16))
    degree, valid = degrees(tile_row, tile_vals, tile_count)
    q_first = jnp.dot(relaid, w_neigh1, preferred_element_type=jnp.float32).astype(jnp.bfloat16)
    agg_first = aggregate(q_first, send_blocks, tile_row, tile_col, tile_vals, valid, degree)
    hidden = jax.nn.relu(jnp.dot(relaid, w_self1, preferred_element_type=jnp.float32) + agg_first).astype(jnp.bfloat16)
    q_second = jnp.dot(hidden, w_neigh2, preferred_element_type=jnp.float32).astype(jnp.bfloat16)
    agg_second = aggregate(q_second, send_blocks, tile_row, tile_col, tile_vals, valid, degree)
    return (jnp.dot(hidden, w_self2, preferred_element_type=jnp.float32) + agg_second).astype(jnp.bfloat16)
```

```python
import jax
import jax.numpy as jnp
from jax import lax
from jax.experimental import pallas as pl
from jax.experimental.pallas import tpu as pltpu
from jax.sharding import PartitionSpec as P

F = 128
H = 256
BLK = 128
ROWS = 4096
TILES = 256
NB = 32
ND = 128
PER = ROWS // ND
SEG = PER + 8
PAIRS = 176
GROUP = 8
UNROLL = 4
BF = jnp.bfloat16
F32 = jnp.float32
I32 = jnp.int32

SMEM = pl.BlockSpec(memory_space=pltpu.SMEM)
VMEM = pl.BlockSpec(memory_space=pltpu.VMEM)
ANY = pl.BlockSpec(memory_space=pl.ANY)


def params(mib):
    return pltpu.CompilerParams(vmem_limit_bytes=mib * 1024 * 1024)


def cost(flops, nbytes):
    return pl.CostEstimate(flops=flops, bytes_accessed=nbytes, transcendentals=0)


def mm(a, b):
    return jnp.dot(a, b, preferred_element_type=F32)


def mm_t(a, b):
    return lax.dot_general(a, b, (((1,), (1,)), ((), ())), preferred_element_type=F32)


def pack_kernel(owner, slot, feat, out, rows, pos_v, pos_s, sem):
    sub = lax.broadcasted_iota(I32, (BLK, BLK), 0)
    lane = lax.broadcasted_iota(I32, (BLK, BLK), 1)
    before = jnp.concatenate([(sub < lane).astype(BF), jnp.ones((BLK, BLK), BF)], axis=1)
    carry = jnp.zeros((BLK, BLK), F32)
    digits = jnp.zeros((BLK, BLK), F32)
    for c in range(ROWS // BLK):
        own = owner[c : c + 1, :]
        hit = own == sub
        hit_f = hit.astype(F32)
        counts = mm(hit_f.astype(BF), before)
        rank = jnp.sum(hit_f * (counts[:, :BLK] + carry), axis=0, keepdims=True)
        carry = carry + counts[:, BLK:]
        rank_i = rank.astype(I32)
        pos_v[c : c + 1, :] = own * SEG + rank_i
        places = slot[c : c + 1, :]
        high = (places >> 6).astype(F32)
        low = (places & 63).astype(F32)
        spread = jnp.concatenate([hit_f * high, hit_f * low], axis=1).astype(BF)
        ranks = jnp.concatenate([rank_i == sub, rank_i + PER == sub], axis=1).astype(F32).astype(BF)
        digits = digits + mm_t(spread, ranks)
    copy = pltpu.make_async_copy(pos_v, pos_s, sem)
    copy.start()
    rows.reshape(ND, SEG, F)[:, PER:, :] = jnp.broadcast_to(digits[:, None, :], (ND, SEG - PER, F))
    copy.wait()

    def move(i, _):
        c = i >> 3
        first = (i & 7) * 16
        for u in range(16):
            rows[pl.ds(pos_s[c, first + u], 1), :] = feat[pl.ds(i * 16 + u, 1), :]
        return 0

    lax.fori_loop(0, ROWS // 16, move, 0)
    out[...] = rows[...].reshape(ND, SEG, F).astype(BF)


def pack(features, owner, slot):
    return pl.pallas_call(
        pack_kernel,
        out_shape=jax.ShapeDtypeStruct((ND, SEG, F), BF),
        in_specs=[VMEM] * 3,
        out_specs=VMEM,
        scratch_shapes=[
            pltpu.VMEM((ND * SEG, F), F32),
            pltpu.VMEM((ROWS // BLK, BLK), I32),
            pltpu.SMEM((ROWS // BLK, BLK), I32),
            pltpu.SemaphoreType.DMA,
        ],
        compiler_params=params(24),
        name="pack",
    )(owner.reshape(ROWS // BLK, BLK), slot.reshape(ROWS // BLK, BLK), features)


def unpack_kernel(send_blocks, arrived, relaid, send, rows, placed, slot_v, slot_s, sem, sem_out):
    rows[...] = arrived[...].astype(F32).reshape(ND * SEG, F)
    digits = rows[pl.ds(PER, ND, stride=SEG), :]
    slot_v[...] = (digits * 64.0 + pltpu.roll(digits, F - PER, 1)).astype(I32)
    copy = pltpu.make_async_copy(slot_v, slot_s, sem)
    copy.start()
    copy.wait()

    def move(i, _):
        for u in range(PER):
            placed[pl.ds(slot_s[i, u], 1), :] = rows[pl.ds(i * SEG + u, 1), :]
        return 0

    lax.fori_loop(0, ND, move, 0)
    relaid[...] = placed[...].reshape(NB, BLK, F).astype(BF)

    def post(d, _):
        pltpu.make_async_copy(relaid.at[send_blocks[d]], send.at[d], sem_out).start()
        return 0

    lax.fori_loop(0, ND, post, 0)
    pltpu.make_async_copy(send, send, sem_out).wait()


def unpack(send_blocks, arrived):
    return pl.pallas_call(
        unpack_kernel,
        out_shape=(
            jax.ShapeDtypeStruct((NB, BLK, F), BF),
            jax.ShapeDtypeStruct((ND, BLK, F), BF),
        ),
        in_specs=[SMEM, VMEM],
        out_specs=(VMEM, ANY),
        scratch_shapes=[
            pltpu.VMEM((ND * SEG, F), F32),
            pltpu.VMEM((ROWS, F), F32),
            pltpu.VMEM((ND, F), I32),
            pltpu.SMEM((ND, F), I32),
            pltpu.SemaphoreType.DMA,
            pltpu.SemaphoreType.DMA,
        ],
        compiler_params=params(24),
        name="unpack",
    )(send_blocks, arrived)


def prepare_kernel(
    row_s, col_s, count_s, send_blocks, tile_vals, relaid,
    pairs, acc_out, inv_out, row_k, col_k, meta, dest, dest_at,
    tiles, acc, held, cursor, tile_k, sem,
):
    load = pltpu.make_async_copy(tile_vals, tiles.at[pl.ds(0, TILES)], sem)
    load.start()
    tiles[TILES] = jnp.zeros((BLK, BLK), I32)
    acc[...] = jnp.zeros_like(acc)

    def clear(i, _):
        cursor[i] = 0
        return 0

    lax.fori_loop(0, 2 * NB, clear, 0)

    def clear_pair(i, _):
        row_k[i] = 0
        for s in (0, 1):
            tile_k[2 * i + s] = TILES
            col_k[2 * i + s] = 0
        return 0

    lax.fori_loop(0, PAIRS, clear_pair, 0)
    used = count_s[0]

    def tally(t, _):
        g = row_s[t] + jnp.where(col_s[t] >= NB, NB, 0)
        cursor[g] = cursor[g] + 1
        return 0

    lax.fori_loop(0, used, tally, 0)

    def starts(g, at):
        n = cursor[g]
        cursor[g] = 2 * at
        return at + ((n + 1) >> 1)

    n_own = lax.fori_loop(0, NB, starts, 0)
    n_own = (n_own + GROUP - 1) // GROUP * GROUP
    n_all = lax.fori_loop(NB, 2 * NB, starts, n_own)
    n_all = (n_all + GROUP - 1) // GROUP * GROUP
    meta[0] = n_own
    meta[1] = n_all

    def place(t, _):
        row = row_s[t]
        col = col_s[t]
        far = col >= NB
        col = jnp.where(far, col - NB, col)
        g = row + jnp.where(far, NB, 0)
        at = cursor[g]
        cursor[g] = at + 1
        tile_k[at] = t
        col_k[at] = col
        row_k[at >> 1] = row
        return 0

    lax.fori_loop(0, used, place, 0)

    def zero_dest(i, _):
        cursor[i] = 0
        return 0

    lax.fori_loop(0, NB, zero_dest, 0)

    def tally_dest(d, _):
        b = send_blocks[d]
        cursor[b] = cursor[b] + 1
        return 0

    lax.fori_loop(0, ND, tally_dest, 0)

    def starts_dest(b, at):
        n = cursor[b]
        cursor[b] = at
        dest_at[b] = at
        return at + n

    dest_at[NB] = lax.fori_loop(0, NB, starts_dest, 0)

    def place_dest(d, _):
        b = send_blocks[d]
        at = cursor[b]
        cursor[b] = at + 1
        dest[at] = d
        return 0

    lax.fori_loop(0, ND, place_dest, 0)
    load.wait()
    ones = jnp.ones((2 * BLK, BLK), BF)

    def fetch(k):
        v = jnp.concatenate([tiles[tile_k[2 * k]], tiles[tile_k[2 * k + 1]]], axis=1)
        v = v.astype(F32).astype(BF)
        pairs[k] = v
        return v

    def own(i, _):
        for u in range(UNROLL):
            k = i * UNROLL + u
            v = fetch(k)
            x = jnp.concatenate([relaid[col_k[2 * k]], relaid[col_k[2 * k + 1]]], axis=0)
            got = mm(v, jnp.concatenate([x, ones], axis=1))
            acc[row_k[k]] += got
        return 0

    lax.fori_loop(0, n_own // UNROLL, own, 0)

    def far(i, _):
        for u in range(UNROLL):
            k = i * UNROLL + u
            r = row_k[k]
            acc[r, :, BLK:] += mm(fetch(k), ones)
        return 0

    lax.fori_loop(n_own // UNROLL, n_all // UNROLL, far, 0)
    acc_out[...] = acc[:, :, :BLK]
    inv_out[...] = 1.0 / jnp.maximum(acc[:, :, BLK:], 1.0)


def prepare(tile_row, tile_col, tile_count, send_blocks, tile_vals, relaid):
    ints = lambda n: jax.ShapeDtypeStruct((n,), I32)
    return pl.pallas_call(
        prepare_kernel,
        out_shape=(
            jax.ShapeDtypeStruct((PAIRS, BLK, 2 * BLK), BF),
            jax.ShapeDtypeStruct((NB, BLK, F), F32),
            jax.ShapeDtypeStruct((NB, BLK, BLK), F32),
            ints(PAIRS),
            ints(2 * PAIRS),
            ints(8),
            ints(ND),
            ints(NB + 8),
        ),
        in_specs=[SMEM, SMEM, SMEM, SMEM, ANY, VMEM],
        out_specs=(VMEM, VMEM, VMEM, SMEM, SMEM, SMEM, SMEM, SMEM),
        scratch_shapes=[
            pltpu.VMEM((TILES + 1, BLK, BLK), I32),
            pltpu.VMEM((NB, BLK, 2 * BLK), F32),
            pltpu.VMEM((8, BLK), F32),
            pltpu.SMEM((2 * NB,), I32),
            pltpu.SMEM((2 * PAIRS,), I32),
            pltpu.SemaphoreType.DMA,
        ],
        compiler_params=params(48),
        cost_estimate=cost(2 * 10**9, 32 * 2**20),
        name="prepare",
    )(tile_row, tile_col, tile_count, send_blocks, tile_vals, relaid)


def add_pairs(first, last, start, held, sems, table, acc, row_k, col_k):
    def group(c, _):
        pltpu.make_async_copy(held.at[pl.ds(0, GROUP)], held.at[pl.ds(0, GROUP)], sems.at[c]).wait()
        for u0 in range(0, GROUP, UNROLL):
            for u in range(u0, u0 + UNROLL):
                k = first + c * GROUP + u
                x = jnp.concatenate([table[col_k[2 * k]], table[col_k[2 * k + 1]]], axis=0)
                got = mm(held[c * GROUP + u], x)
                acc[row_k[k]] += got
        return 0

    lax.fori_loop(0, (last - first) // GROUP, group, 0)


def load_pairs(first, last, pairs, held, sems):
    def group(c, _):
        pltpu.make_async_copy(
            pairs.at[pl.ds(first + c * GROUP, GROUP)], held.at[pl.ds(c * GROUP, GROUP)], sems.at[c]
        ).start()
        return 0

    lax.fori_loop(0, (last - first) // GROUP, group, 0)


def first_kernel(
    row_k, col_k, meta, dest, dest_at, pairs, remote, relaid, acc_in, inv, w_self, w_neigh, w_next,
    hidden, q_out, send,
    held, acc, sems, sem_out,
):
    n_own = meta[0]
    n_all = meta[1]
    load_pairs(n_own, n_all, pairs, held, sems)
    acc[...] = acc_in[...]
    add_pairs(n_own, n_all, 0, held, sems, remote, acc, row_k, col_k)
    weights = jnp.concatenate([w_self[...], w_neigh[...], w_neigh[...]], axis=0)

    def finish(i, _):
        b = pl.ds(2 * i, 2)
        mean = (acc[b] * inv[b]).reshape(2 * BLK, F)
        high = mean.astype(BF)
        low = (mean - high.astype(F32)).astype(BF)
        x = jnp.concatenate([relaid[b].reshape(2 * BLK, F), high, low], axis=1)
        h = jnp.maximum(mm(x, weights), 0.0).astype(BF)
        hidden[b] = h.reshape(2, BLK, H)
        q_out[b] = mm(h, w_next[...]).astype(BF).reshape(2, BLK, H)

        def post(j, _):
            d = dest[j]
            blk = 2 * i + jnp.where(j >= dest_at[2 * i + 1], 1, 0)
            pltpu.make_async_copy(q_out.at[blk], send.at[d], sem_out).start()
            return 0

        lax.fori_loop(dest_at[2 * i], dest_at[2 * i + 2], post, 0)
        return 0

    lax.fori_loop(0, NB // 2, finish, 0)
    pltpu.make_async_copy(send, send, sem_out).wait()


def first(lists, pairs, remote, relaid, acc, inv, w_self, w_neigh, w_next):
    row_k, col_k, meta, dest, dest_at = lists
    return pl.pallas_call(
        first_kernel,
        out_shape=(
            jax.ShapeDtypeStruct((NB, BLK, H), BF),
            jax.ShapeDtypeStruct((NB, BLK, H), BF),
            jax.ShapeDtypeStruct((ND, BLK, H), BF),
        ),
        in_specs=[SMEM] * 5 + [ANY] + [VMEM] * 7,
        out_specs=(VMEM, VMEM, ANY),
        scratch_shapes=[
            pltpu.VMEM((PAIRS, BLK, 2 * BLK), BF),
            pltpu.VMEM((NB, BLK, F), F32),
            pltpu.SemaphoreType.DMA((PAIRS // GROUP,)),
            pltpu.SemaphoreType.DMA,
        ],
        compiler_params=params(48),
        name="first_layer",
    )(row_k, col_k, meta, dest, dest_at, pairs, remote, relaid, acc, inv, w_self, w_neigh, w_next)


def own_kernel(row_k, col_k, meta, pairs, q, hidden, inv, w_self, base, held, acc, sems):
    n_own = meta[0]
    load_pairs(0, n_own, pairs, held, sems)
    acc[...] = jnp.zeros_like(acc)
    add_pairs(0, n_own, 0, held, sems, q, acc, row_k, col_k)

    def finish(b, _):
        scale = inv[b]
        base[b] = mm(hidden[b], w_self[...]) + acc[b] * jnp.concatenate([scale, scale], axis=1)
        return 0

    lax.fori_loop(0, NB, finish, 0)


def own_part(lists, pairs, q, hidden, inv, w_self):
    row_k, col_k, meta, _, _ = lists
    return pl.pallas_call(
        own_kernel,
        out_shape=jax.ShapeDtypeStruct((NB, BLK, H), F32),
        in_specs=[SMEM] * 3 + [ANY] + [VMEM] * 4,
        out_specs=VMEM,
        scratch_shapes=[
            pltpu.VMEM((PAIRS, BLK, 2 * BLK), BF),
            pltpu.VMEM((NB, BLK, H), F32),
            pltpu.SemaphoreType.DMA((PAIRS // GROUP,)),
        ],
        compiler_params=params(48),
        cost_estimate=cost(2 * 10**9, 32 * 2**20),
        name="own_part",
    )(row_k, col_k, meta, pairs, q, hidden, inv, w_self)


def second_kernel(row_k, col_k, meta, pairs, remote, base, inv, out, held, acc, sems):
    n_own = meta[0]
    n_all = meta[1]
    load_pairs(n_own, n_all, pairs, held, sems)
    acc[...] = jnp.zeros_like(acc)
    add_pairs(n_own, n_all, 0, held, sems, remote, acc, row_k, col_k)

    def finish(b, _):
        scale = inv[b]
        out[b] = (base[b] + acc[b] * jnp.concatenate([scale, scale], axis=1)).astype(BF)
        return 0

    lax.fori_loop(0, NB, finish, 0)


def second(lists, pairs, remote, base, inv):
    row_k, col_k, meta, _, _ = lists
    return pl.pallas_call(
        second_kernel,
        out_shape=jax.ShapeDtypeStruct((NB, BLK, H), BF),
        in_specs=[SMEM] * 3 + [ANY] + [VMEM] * 3,
        out_specs=VMEM,
        scratch_shapes=[
            pltpu.VMEM((PAIRS, BLK, 2 * BLK), BF),
            pltpu.VMEM((NB, BLK, H), F32),
            pltpu.SemaphoreType.DMA((PAIRS // GROUP,)),
        ],
        compiler_params=params(48),
        name="second_layer",
    )(row_k, col_k, meta, pairs, remote, base, inv)


def exchange(x):
    return lax.all_to_all(x, "dom", split_axis=0, concat_axis=0, tiled=True)


def local(
    features, owner, slot, send_blocks, tile_row, tile_col, tile_vals, tile_count,
    w_self1, w_neigh1, w_self2, w_neigh2,
):
    picks = send_blocks.reshape(ND)
    arrived = exchange(pack(features, owner, slot))
    relaid, send = unpack(picks, arrived)
    remote = exchange(send)
    pairs, acc, inv, *lists = prepare(tile_row, tile_col, tile_count, picks, tile_vals, relaid)
    hidden, q, send = first(lists, pairs, remote, relaid, acc, inv, w_self1, w_neigh1, w_neigh2)
    remote = exchange(send)
    base = own_part(lists, pairs, q, hidden, inv, w_self2)
    return second(lists, pairs, remote, base, inv).reshape(ROWS, H)


def solution(mesh):
    rows, flat = P("dom", None), P("dom")
    cube = P("dom", None, None)
    placed = (rows, flat, flat, cube, flat, flat, cube, flat, P(), P(), P(), P())
    return jax.shard_map(local, mesh=mesh, in_specs=placed, out_specs=rows, check_vma=False)
```

```python
import jax
import jax.numpy as jnp
from jax import lax
from jax.experimental import pallas as pl
from jax.experimental.pallas import tpu as pltpu
from jax.sharding import PartitionSpec as P

F = 128
H = 256
BLK = 128
ROWS = 4096
TILES = 256
NB = 32
ND = 128
PER = ROWS // ND
SEG = PER + 8
PAIRS = 176
GROUP = 8
BATCH = 8
BATCHES = NB // BATCH
UNROLL = 4
BF = jnp.bfloat16
F32 = jnp.float32
I32 = jnp.int32

SMEM = pl.BlockSpec(memory_space=pltpu.SMEM)
VMEM = pl.BlockSpec(memory_space=pltpu.VMEM)
ANY = pl.BlockSpec(memory_space=pl.ANY)


def params(mib):
    return pltpu.CompilerParams(vmem_limit_bytes=mib * 1024 * 1024)


def cost(flops, nbytes):
    return pl.CostEstimate(flops=flops, bytes_accessed=nbytes, transcendentals=0)


def mm(a, b):
    return jnp.dot(a, b, preferred_element_type=F32)


def mm_t(a, b):
    return lax.dot_general(a, b, (((1,), (1,)), ((), ())), preferred_element_type=F32)


def pack_kernel(owner, slot, feat, out, rows, held, pos_v, pos_s, sem, sem_feat):
    load = pltpu.make_async_copy(feat, held, sem_feat)
    load.start()
    sub = lax.broadcasted_iota(I32, (BLK, BLK), 0)
    lane = lax.broadcasted_iota(I32, (BLK, BLK), 1)
    before = jnp.concatenate([(sub < lane).astype(BF), jnp.ones((BLK, BLK), BF)], axis=1)
    carry = jnp.zeros((BLK, BLK), F32)
    digits = jnp.zeros((BLK, BLK), F32)
    for c in range(ROWS // BLK):
        own = owner[c : c + 1, :]
        hit = own == sub
        hit_f = hit.astype(F32)
        counts = mm(hit_f.astype(BF), before)
        rank = jnp.sum(hit_f * (counts[:, :BLK] + carry), axis=0, keepdims=True)
        carry = carry + counts[:, BLK:]
        rank_i = rank.astype(I32)
        pos_v[c : c + 1, :] = own * SEG + rank_i
        places = slot[c : c + 1, :]
        high = (places >> 6).astype(F32)
        low = (places & 63).astype(F32)
        spread = jnp.concatenate([hit_f * high, hit_f * low], axis=1).astype(BF)
        ranks = jnp.concatenate([rank_i == sub, rank_i + PER == sub], axis=1).astype(F32).astype(BF)
        digits = digits + mm_t(spread, ranks)
    copy = pltpu.make_async_copy(pos_v, pos_s, sem)
    copy.start()
    rows.reshape(ND, SEG, F)[:, PER:, :] = jnp.broadcast_to(digits[:, None, :], (ND, SEG - PER, F))
    copy.wait()
    load.wait()

    def move(c, _):
        for u in range(BLK):
            rows[pl.ds(pos_s[c, u], 1), :] = held[pl.ds(c * BLK + u, 1), :]
        return 0

    lax.fori_loop(0, ROWS // BLK, move, 0)
    out[...] = rows[...].reshape(ND, SEG, F).astype(BF)


def pack(features, owner, slot):
    return pl.pallas_call(
        pack_kernel,
        out_shape=jax.ShapeDtypeStruct((ND, SEG, F), BF),
        in_specs=[VMEM, VMEM, ANY],
        out_specs=VMEM,
        scratch_shapes=[
            pltpu.VMEM((ND * SEG, F), F32),
            pltpu.VMEM((ROWS, F), F32),
            pltpu.VMEM((ROWS // BLK, BLK), I32),
            pltpu.SMEM((ROWS // BLK, BLK), I32),
            pltpu.SemaphoreType.DMA,
            pltpu.SemaphoreType.DMA,
        ],
        compiler_params=params(56),
        name="pack",
    )(owner.reshape(ROWS // BLK, BLK), slot.reshape(ROWS // BLK, BLK), features)


def unpack_kernel(send_blocks, arrived, relaid, send, rows, placed, slot_v, slot_s, sem, sem_out):
    rows[...] = arrived[...].astype(F32).reshape(ND * SEG, F)
    digits = rows[pl.ds(PER, ND, stride=SEG), :]
    slots = digits * 64.0 + pltpu.roll(digits, F - PER, 1)
    lane = lax.broadcasted_iota(I32, (PER, F), 1)
    slots = [jnp.where(lane < PER, slots[PER * g : PER * (g + 1)], 0.0) for g in range(ND // PER)]
    slots = [slots[0]] + [pltpu.roll(slots[g], PER * g, 1) for g in range(1, ND // PER)]
    slot_v[...] = sum(slots).astype(I32)
    copy = pltpu.make_async_copy(slot_v, slot_s, sem)
    copy.start()
    copy.wait()

    def move(i, _):
        for u in range(F):
            source = (i + PER * (u // PER)) * SEG + u % PER
            placed[pl.ds(slot_s[i, u], 1), :] = rows[pl.ds(source, 1), :]
        return 0

    lax.fori_loop(0, PER, move, 0)
    relaid[...] = placed[...].reshape(NB, BLK, F).astype(BF)

    def post(d, _):
        pltpu.make_async_copy(relaid.at[send_blocks[d]], send.at[d], sem_out).start()
        return 0

    lax.fori_loop(0, ND, post, 0)
    pltpu.make_async_copy(send, send, sem_out).wait()


def unpack(send_blocks, arrived):
    return pl.pallas_call(
        unpack_kernel,
        out_shape=(
            jax.ShapeDtypeStruct((NB, BLK, F), BF),
            jax.ShapeDtypeStruct((ND, BLK, F), BF),
        ),
        in_specs=[SMEM, VMEM],
        out_specs=(VMEM, ANY),
        scratch_shapes=[
            pltpu.VMEM((ND * SEG, F), F32),
            pltpu.VMEM((ROWS, F), F32),
            pltpu.VMEM((PER, F), I32),
            pltpu.SMEM((PER, F), I32),
            pltpu.SemaphoreType.DMA,
            pltpu.SemaphoreType.DMA,
        ],
        compiler_params=params(56),
        name="unpack",
    )(send_blocks, arrived)


def prepare_kernel(
    row_s, col_s, count_s, send_blocks, tile_vals, relaid,
    pairs, base, inv_out, row_k, col_k, meta, dest, dest_at,
    tiles, acc, held, cursor, tile_k, sem,
):
    load = pltpu.make_async_copy(tile_vals, tiles.at[pl.ds(0, TILES)], sem)
    load.start()
    tiles[TILES] = jnp.zeros((BLK, BLK), I32)
    acc[...] = jnp.zeros_like(acc)

    def clear(i, _):
        cursor[i] = 0
        return 0

    lax.fori_loop(0, 2 * NB, clear, 0)

    def clear_pair(i, _):
        row_k[i] = 0
        for s in (0, 1):
            tile_k[2 * i + s] = TILES
            col_k[2 * i + s] = 0
        return 0

    lax.fori_loop(0, PAIRS, clear_pair, 0)
    used = count_s[0]

    def tally(t, _):
        g = row_s[t] + jnp.where(col_s[t] >= NB, NB, 0)
        cursor[g] = cursor[g] + 1
        return 0

    lax.fori_loop(0, used, tally, 0)

    def starts(g, at):
        n = cursor[g]
        cursor[g] = 2 * at
        return at + ((n + 1) >> 1)

    n_own = lax.fori_loop(0, NB, starts, 0)
    n_own = (n_own + GROUP - 1) // GROUP * GROUP
    n_all = lax.fori_loop(NB, 2 * NB, starts, n_own)
    n_all = (n_all + GROUP - 1) // GROUP * GROUP
    meta[0] = n_own
    meta[1] = n_all

    def place(t, _):
        row = row_s[t]
        col = col_s[t]
        far = col >= NB
        col = jnp.where(far, col - NB, col)
        g = row + jnp.where(far, NB, 0)
        at = cursor[g]
        cursor[g] = at + 1
        tile_k[at] = t
        col_k[at] = col
        row_k[at >> 1] = row
        return 0

    lax.fori_loop(0, used, place, 0)

    def zero_dest(i, _):
        cursor[i] = 0
        return 0

    lax.fori_loop(0, NB, zero_dest, 0)

    def tally_dest(d, _):
        b = send_blocks[d]
        cursor[b] = cursor[b] + 1
        return 0

    lax.fori_loop(0, ND, tally_dest, 0)

    def starts_dest(b, at):
        n = cursor[b]
        cursor[b] = at
        dest_at[b] = at
        return at + n

    dest_at[NB] = lax.fori_loop(0, NB, starts_dest, 0)

    def place_dest(d, _):
        b = send_blocks[d]
        at = cursor[b]
        cursor[b] = at + 1
        dest[at] = d
        return 0

    lax.fori_loop(0, ND, place_dest, 0)
    load.wait()
    ones = jnp.ones((2 * BLK, BLK), BF)

    def fetch(k):
        v = jnp.concatenate([tiles[tile_k[2 * k]], tiles[tile_k[2 * k + 1]]], axis=1)
        v = v.astype(F32).astype(BF)
        pairs[k] = v
        return v

    def own(i, _):
        for u in range(UNROLL):
            k = i * UNROLL + u
            v = fetch(k)
            x = jnp.concatenate([relaid[col_k[2 * k]], relaid[col_k[2 * k + 1]]], axis=0)
            got = mm(v, jnp.concatenate([x, ones], axis=1))
            acc[row_k[k]] += got
        return 0

    lax.fori_loop(0, n_own // UNROLL, own, 0)

    def far(i, _):
        for u in range(UNROLL):
            k = i * UNROLL + u
            r = row_k[k]
            acc[r, :, BLK:] += mm(fetch(k), ones)
        return 0

    lax.fori_loop(n_own // UNROLL, n_all // UNROLL, far, 0)
    inv = 1.0 / jnp.maximum(acc[:, :, BLK:], 1.0)
    inv_out[...] = inv
    base[...] = acc[:, :, :BLK] * inv


def prepare(tile_row, tile_col, tile_count, send_blocks, tile_vals, relaid):
    ints = lambda n: jax.ShapeDtypeStruct((n,), I32)
    return pl.pallas_call(
        prepare_kernel,
        out_shape=(
            jax.ShapeDtypeStruct((PAIRS, BLK, 2 * BLK), BF),
            jax.ShapeDtypeStruct((NB, BLK, F), F32),
            jax.ShapeDtypeStruct((NB, BLK, BLK), F32),
            ints(PAIRS),
            ints(2 * PAIRS),
            ints(8),
            ints(ND),
            ints(NB + 8),
        ),
        in_specs=[SMEM, SMEM, SMEM, SMEM, ANY, VMEM],
        out_specs=(VMEM, VMEM, VMEM, SMEM, SMEM, SMEM, SMEM, SMEM),
        scratch_shapes=[
            pltpu.VMEM((TILES + 1, BLK, BLK), I32),
            pltpu.VMEM((NB, BLK, 2 * BLK), F32),
            pltpu.VMEM((8, BLK), F32),
            pltpu.SMEM((2 * NB,), I32),
            pltpu.SMEM((2 * PAIRS,), I32),
            pltpu.SemaphoreType.DMA,
        ],
        compiler_params=params(56),
        cost_estimate=cost(2 * 10**9, 32 * 2**20),
        name="prepare",
    )(tile_row, tile_col, tile_count, send_blocks, tile_vals, relaid)


def load_pairs(first, last, pairs, held, sems, begin=0, end=PAIRS):
    def group(c, _):
        pltpu.make_async_copy(
            pairs.at[pl.ds(first + c * GROUP, GROUP)], held.at[pl.ds(c * GROUP, GROUP)], sems.at[c]
        ).start()
        return 0

    groups = (last - first) // GROUP
    lax.fori_loop(jnp.minimum(begin, groups), jnp.minimum(end, groups), group, 0)


def row_copies(i, base, inv, base_v, inv_v, sems_base, sems_inv):
    b = pl.ds(BATCH * i, BATCH)
    return (
        pltpu.make_async_copy(base.at[b], base_v.at[b], sems_base.at[i]),
        pltpu.make_async_copy(inv.at[b], inv_v.at[b], sems_inv.at[i]),
    )


def add_pairs(first, last, held, sems, table, acc, row_k, col_k, finish):
    groups = (last - first) // GROUP

    def group(c, done):
        pltpu.make_async_copy(held.at[pl.ds(0, GROUP)], held.at[pl.ds(0, GROUP)], sems.at[c]).wait()
        for u0 in range(0, GROUP, UNROLL):
            for u in range(u0, u0 + UNROLL):
                k = first + c * GROUP + u
                x = jnp.concatenate([table[col_k[2 * k]], table[col_k[2 * k + 1]]], axis=0)
                got = mm(held[c * GROUP + u], x)
                acc[row_k[k]] += got
        following = row_k[jnp.minimum(first + (c + 1) * GROUP, PAIRS - 1)]
        upto = jnp.where(c + 1 < groups, following, NB) // BATCH
        lax.fori_loop(done, upto, finish, 0)
        return upto

    lax.fori_loop(lax.fori_loop(0, groups, group, 0), BATCHES, finish, 0)


def first_kernel(
    row_k, col_k, meta, dest, dest_at, remote, pairs, base, inv, mean_out, send,
    table, held, base_v, inv_v, acc, mean, sems, sems_base, sems_inv, sem_table, sem_mean, sem_out,
):
    load_table = pltpu.make_async_copy(remote, table, sem_table)
    rows = lambda i: row_copies(i, base, inv, base_v, inv_v, sems_base, sems_inv)

    def load(i, _):
        load_pairs(meta[0], meta[1], pairs, held, sems, 2 * i, 2 * i + 2)
        for copy in rows(i):
            copy.start()
        return 0

    load_table.start()
    lax.fori_loop(0, EARLY, load, 0)
    acc[...] = jnp.zeros_like(acc)
    load_table.wait()
    lax.fori_loop(EARLY, BATCHES, load, 0)
    load_pairs(meta[0], meta[1], pairs, held, sems, 2 * BATCHES)

    def finish(i, _):
        for copy in rows(i):
            copy.wait()
        b = pl.ds(BATCH * i, BATCH)
        mean[b] = (base_v[b] + acc[b] * inv_v[b]).astype(BF)
        pltpu.make_async_copy(mean.at[b], mean_out.at[b], sem_mean).start()

        def post(j, blk):
            blk = lax.while_loop(lambda at: j >= dest_at[at + 1], lambda at: at + 1, blk)
            pltpu.make_async_copy(mean.at[blk], send.at[dest[j]], sem_out).start()
            return blk

        lax.fori_loop(dest_at[BATCH * i], dest_at[BATCH * (i + 1)], post, BATCH * i)
        return 0

    add_pairs(meta[0], meta[1], held, sems, table, acc, row_k, col_k, finish)
    pltpu.make_async_copy(mean_out, mean_out, sem_mean).wait()
    pltpu.make_async_copy(send, send, sem_out).wait()


def first(lists, pairs, remote, base, inv):
    row_k, col_k, meta, dest, dest_at = lists
    return pl.pallas_call(
        first_kernel,
        out_shape=(
            jax.ShapeDtypeStruct((NB, BLK, F), BF),
            jax.ShapeDtypeStruct((ND, BLK, F), BF),
        ),
        in_specs=[SMEM] * 5 + [ANY] * 4,
        out_specs=(ANY, ANY),
        scratch_shapes=[
            pltpu.VMEM((ND, BLK, F), BF),
            pltpu.VMEM((PAIRS, BLK, 2 * BLK), BF),
            pltpu.VMEM((NB, BLK, F), F32),
            pltpu.VMEM((NB, BLK, BLK), F32),
            pltpu.VMEM((NB, BLK, F), F32),
            pltpu.VMEM((NB, BLK, F), BF),
            pltpu.SemaphoreType.DMA((PAIRS // GROUP,)),
            pltpu.SemaphoreType.DMA((BATCHES,)),
            pltpu.SemaphoreType.DMA((BATCHES,)),
        ]
        + [pltpu.SemaphoreType.DMA] * 3,
        compiler_params=params(56),
        name="first_layer",
    )(row_k, col_k, meta, dest, dest_at, remote, pairs, base, inv)


def own_kernel(
    row_k, col_k, meta, pairs, relaid, mean, inv, w_self1, w_neigh1, w_self2, w_neigh2, base,
    hidden, acc, held, sems,
):
    load_pairs(0, meta[0], pairs, held, sems)
    acc[...] = jnp.zeros_like(acc)
    weights = jnp.concatenate([w_self1[...], w_neigh1[...]], axis=0)
    final = jnp.concatenate([w_self2[...], w_neigh2[...], w_neigh2[...]], axis=0)

    def layer(i, _):
        b = pl.ds(2 * i, 2)
        x = jnp.concatenate([relaid[b].reshape(2 * BLK, F), mean[b].reshape(2 * BLK, F)], axis=1)
        hidden[b] = jnp.maximum(mm(x, weights), 0.0).astype(BF).reshape(2, BLK, H)
        return 0

    lax.fori_loop(0, NB // 2, layer, 0)

    def finish(i, _):
        b = pl.ds(BATCH * i, BATCH)
        scale = inv[b].reshape(BATCH * BLK, BLK)
        m = acc[b].reshape(BATCH * BLK, H) * jnp.concatenate([scale, scale], axis=1)
        high = m.astype(BF)
        low = (m - high.astype(F32)).astype(BF)
        x = jnp.concatenate([hidden[b].reshape(BATCH * BLK, H), high, low], axis=1)
        base[b] = mm(x, final).reshape(BATCH, BLK, H)
        return 0

    add_pairs(0, meta[0], held, sems, hidden, acc, row_k, col_k, finish)


def own_part(lists, pairs, relaid, mean, inv, w_self1, w_neigh1, w_self2, w_neigh2):
    row_k, col_k, meta, _, _ = lists
    return pl.pallas_call(
        own_kernel,
        out_shape=jax.ShapeDtypeStruct((NB, BLK, H), F32),
        in_specs=[SMEM] * 3 + [ANY] + [VMEM] * 7,
        out_specs=VMEM,
        scratch_shapes=[
            pltpu.VMEM((NB, BLK, H), BF),
            pltpu.VMEM((NB, BLK, H), F32),
            pltpu.VMEM((PAIRS, BLK, 2 * BLK), BF),
            pltpu.SemaphoreType.DMA((PAIRS // GROUP,)),
        ],
        compiler_params=params(56),
        cost_estimate=cost(2 * 10**9, 32 * 2**20),
        name="own_part",
    )(row_k, col_k, meta, pairs, relaid, mean, inv, w_self1, w_neigh1, w_self2, w_neigh2)


EARLY = 2
CHUNK = ND // BATCHES


def second_kernel(
    row_k, col_k, meta, near, far, pairs, base, inv, w_self1, w_neigh1, w_neigh2, out,
    near_v, far_v, table, held, base_v, inv_v, acc, result,
    sems, sems_near, sems_far, sems_base, sems_inv, sem_out,
):
    def chunk(c):
        part = pl.ds(c * CHUNK, CHUNK)
        return (
            pltpu.make_async_copy(near.at[part], near_v.at[part], sems_near.at[c]),
            pltpu.make_async_copy(far.at[part], far_v.at[part], sems_far.at[c]),
        )

    rows = lambda i: row_copies(i, base, inv, base_v, inv_v, sems_base, sems_inv)

    def load(i):
        load_pairs(meta[0], meta[1], pairs, held, sems, 2 * i, 2 * i + 2)
        for copy in rows(i):
            copy.start()

    for c in range(ND // CHUNK):
        for copy in chunk(c):
            copy.start()
    acc[...] = jnp.zeros_like(acc)
    weights = jnp.concatenate([w_self1[...], w_neigh1[...]], axis=0)

    def layer(c, _):
        for copy in chunk(c):
            copy.wait()
        load(c)
        for i in range(CHUNK // 2):
            b = pl.ds(c * CHUNK + 2 * i, 2)
            x = jnp.concatenate([near_v[b].reshape(2 * BLK, F), far_v[b].reshape(2 * BLK, F)], axis=1)
            table[b] = jnp.maximum(mm(x, weights), 0.0).astype(BF).reshape(2, BLK, H)
        return 0

    lax.fori_loop(0, BATCHES, layer, 0)
    load_pairs(meta[0], meta[1], pairs, held, sems, 2 * BATCHES)

    def finish(i, _):
        for copy in rows(i):
            copy.wait()
        b = pl.ds(BATCH * i, BATCH)
        scale = inv_v[b].reshape(BATCH * BLK, BLK)
        m = acc[b].reshape(BATCH * BLK, H) * jnp.concatenate([scale, scale], axis=1)
        total = base_v[b].reshape(BATCH * BLK, H) + mm(m.astype(BF), w_neigh2[...])
        result[b] = total.astype(BF).reshape(BATCH, BLK, H)
        pltpu.make_async_copy(result.at[b], out.at[b], sem_out).start()
        return 0

    add_pairs(meta[0], meta[1], held, sems, table, acc, row_k, col_k, finish)
    pltpu.make_async_copy(out, out, sem_out).wait()


def second(lists, near, far, pairs, base, inv, w_self1, w_neigh1, w_neigh2):
    row_k, col_k, meta, _, _ = lists
    return pl.pallas_call(
        second_kernel,
        out_shape=jax.ShapeDtypeStruct((NB, BLK, H), BF),
        in_specs=[SMEM] * 3 + [ANY] * 5 + [VMEM] * 3,
        out_specs=ANY,
        scratch_shapes=[
            pltpu.VMEM((ND, BLK, F), BF),
            pltpu.VMEM((ND, BLK, F), BF),
            pltpu.VMEM((ND, BLK, H), BF),
            pltpu.VMEM((PAIRS, BLK, 2 * BLK), BF),
            pltpu.VMEM((NB, BLK, H), F32),
            pltpu.VMEM((NB, BLK, BLK), F32),
            pltpu.VMEM((NB, BLK, H), F32),
            pltpu.VMEM((NB, BLK, H), BF),
            pltpu.SemaphoreType.DMA((PAIRS // GROUP,)),
        ]
        + [pltpu.SemaphoreType.DMA((BATCHES,))] * 4
        + [pltpu.SemaphoreType.DMA],
        compiler_params=params(56),
        name="second_layer",
    )(row_k, col_k, meta, near, far, pairs, base, inv, w_self1, w_neigh1, w_neigh2)


def exchange(x):
    return lax.all_to_all(x, "dom", split_axis=0, concat_axis=0, tiled=True)


def local(
    features, owner, slot, send_blocks, tile_row, tile_col, tile_vals, tile_count,
    w_self1, w_neigh1, w_self2, w_neigh2,
):
    picks = send_blocks.reshape(ND)
    arrived = exchange(pack(features, owner, slot))
    relaid, send = unpack(picks, arrived)
    near = exchange(send)
    pairs, base, inv, *lists = prepare(tile_row, tile_col, tile_count, picks, tile_vals, relaid)
    mean, send = first(lists, pairs, near, base, inv)
    far = exchange(send)
    base = own_part(lists, pairs, relaid, mean, inv, w_self1, w_neigh1, w_self2, w_neigh2)
    return second(lists, near, far, pairs, base, inv, w_self1, w_neigh1, w_neigh2).reshape(ROWS, H)


def solution(mesh):
    rows, flat = P("dom", None), P("dom")
    cube = P("dom", None, None)
    placed = (rows, flat, flat, cube, flat, flat, cube, flat, P(), P(), P(), P())
    return jax.shard_map(local, mesh=mesh, in_specs=placed, out_specs=rows, check_vma=False)
```

```python
import jax
import jax.numpy as jnp
from jax import lax
from jax.experimental import pallas as pl
from jax.experimental.pallas import tpu as pltpu
from jax.sharding import PartitionSpec as P

F = 128
H = 256
BLK = 128
ROWS = 4096
TILES = 256
NB = 32
ND = 128
PER = ROWS // ND
SEG = PER + 8
PAIRS = 192
GROUP = 16
BATCH = 8
BATCHES = NB // BATCH
UNROLL = 4
ROW, COL, META, DEST, DEST_AT, LISTS = 0, PAIRS, 3 * PAIRS, 3 * PAIRS + 8, 3 * PAIRS + 136, 1024
BF = jnp.bfloat16
F32 = jnp.float32
I32 = jnp.int32

SMEM = pl.BlockSpec(memory_space=pltpu.SMEM)
VMEM = pl.BlockSpec(memory_space=pltpu.VMEM)
ANY = pl.BlockSpec(memory_space=pl.ANY)


def params(mib):
    return pltpu.CompilerParams(vmem_limit_bytes=mib * 1024 * 1024)


def cost(flops, nbytes):
    return pl.CostEstimate(flops=flops, bytes_accessed=nbytes, transcendentals=0)


def mm(a, b):
    return jnp.dot(a, b, preferred_element_type=F32)


def mm_t(a, b):
    return lax.dot_general(a, b, (((1,), (1,)), ((), ())), preferred_element_type=F32)


def pack_kernel(owner_in, slot_in, feat, out, rows, held, owner, slot, pos_v, pos_s, sem, sem_feat, sem_owner, sem_slot):
    load_owner = pltpu.make_async_copy(owner_in, owner, sem_owner)
    load_slot = pltpu.make_async_copy(slot_in, slot, sem_slot)
    load = pltpu.make_async_copy(feat, held, sem_feat)
    load_owner.start()
    load_slot.start()
    load.start()
    sub = lax.broadcasted_iota(I32, (BLK, BLK), 0)
    lane = lax.broadcasted_iota(I32, (BLK, BLK), 1)
    before = jnp.concatenate([(sub < lane).astype(BF), jnp.ones((BLK, BLK), BF)], axis=1)
    carry = jnp.zeros((BLK, BLK), F32)
    digits = jnp.zeros((BLK, BLK), F32)
    load_owner.wait()
    load_slot.wait()
    for c in range(ROWS // BLK):
        own = owner[c : c + 1, :]
        hit = own == sub
        hit_f = hit.astype(F32)
        counts = mm(hit_f.astype(BF), before)
        rank = jnp.sum(hit_f * (counts[:, :BLK] + carry), axis=0, keepdims=True)
        carry = carry + counts[:, BLK:]
        rank_i = rank.astype(I32)
        pos_v[c : c + 1, :] = own * SEG + rank_i
        places = slot[c : c + 1, :]
        high = (places >> 6).astype(F32)
        low = (places & 63).astype(F32)
        spread = jnp.concatenate([hit_f * high, hit_f * low], axis=1).astype(BF)
        ranks = jnp.concatenate([rank_i == sub, rank_i + PER == sub], axis=1).astype(F32).astype(BF)
        digits = digits + mm_t(spread, ranks)
    copy = pltpu.make_async_copy(pos_v, pos_s, sem)
    copy.start()
    rows.reshape(ND, SEG, F)[:, PER:, :] = jnp.broadcast_to(digits[:, None, :], (ND, SEG - PER, F))
    copy.wait()
    load.wait()

    def move(c, _):
        for u in range(BLK):
            rows[pl.ds(pos_s[c, u], 1), :] = held[pl.ds(c * BLK + u, 1), :]
        return 0

    lax.fori_loop(0, ROWS // BLK, move, 0)
    out[...] = rows[...].reshape(ND, SEG, F).astype(BF)


def pack(features, owner, slot):
    return pl.pallas_call(
        pack_kernel,
        out_shape=jax.ShapeDtypeStruct((ND, SEG, F), BF),
        in_specs=[ANY] * 3,
        out_specs=VMEM,
        scratch_shapes=[
            pltpu.VMEM((ND * SEG, F), F32),
            pltpu.VMEM((ROWS, F), F32),
            pltpu.VMEM((ROWS // BLK, BLK), I32),
            pltpu.VMEM((ROWS // BLK, BLK), I32),
            pltpu.VMEM((ROWS // BLK, BLK), I32),
            pltpu.SMEM((ROWS // BLK, BLK), I32),
        ]
        + [pltpu.SemaphoreType.DMA] * 4,
        compiler_params=params(56),
        name="pack",
    )(owner.reshape(ROWS // BLK, BLK), slot.reshape(ROWS // BLK, BLK), features)


PARTS = 4


def unpack_kernel(
    send_in, arrived, relaid_out, send,
    send_blocks, held, rows, placed, relaid, slot_v, slot_s, sem, sem_send, sems, sem_relaid, sem_out,
):
    part = lambda i: pl.ds(i * (ND // PARTS), ND // PARTS)
    loads = [pltpu.make_async_copy(arrived.at[part(i)], held.at[part(i)], sems.at[i]) for i in range(PARTS)]
    load_send = pltpu.make_async_copy(send_in, send_blocks, sem_send)
    for load in loads:
        load.start()
    load_send.start()
    for i, load in enumerate(loads):
        load.wait()
        size = ND // PARTS * SEG
        rows[pl.ds(i * size, size), :] = held[part(i)].astype(F32).reshape(size, F)
    digits = rows[pl.ds(PER, ND, stride=SEG), :]
    slots = digits * 64.0 + pltpu.roll(digits, F - PER, 1)
    lane = lax.broadcasted_iota(I32, (PER, F), 1)
    slots = [jnp.where(lane < PER, slots[PER * g : PER * (g + 1)], 0.0) for g in range(ND // PER)]
    slots = [slots[0]] + [pltpu.roll(slots[g], PER * g, 1) for g in range(1, ND // PER)]
    slot_v[...] = sum(slots).astype(I32)
    copy = pltpu.make_async_copy(slot_v, slot_s, sem)
    copy.start()
    copy.wait()

    def move(i, _):
        for u in range(F):
            source = (i + PER * (u // PER)) * SEG + u % PER
            placed[pl.ds(slot_s[i, u], 1), :] = rows[pl.ds(source, 1), :]
        return 0

    lax.fori_loop(0, PER, move, 0)
    relaid[...] = placed[...].reshape(NB, BLK, F).astype(BF)
    load_send.wait()

    def post(d, _):
        pltpu.make_async_copy(relaid.at[send_blocks[d]], send.at[d], sem_out).start()
        return 0

    lax.fori_loop(0, ND, post, 0)
    keep = pltpu.make_async_copy(relaid, relaid_out, sem_relaid)
    keep.start()
    pltpu.make_async_copy(send, send, sem_out).wait()
    keep.wait()


def unpack(send_blocks, arrived):
    return pl.pallas_call(
        unpack_kernel,
        out_shape=(
            jax.ShapeDtypeStruct((NB, BLK, F), BF),
            jax.ShapeDtypeStruct((ND, BLK, F), BF),
        ),
        in_specs=[ANY, ANY],
        out_specs=(ANY, ANY),
        scratch_shapes=[
            pltpu.SMEM((ND,), I32),
            pltpu.VMEM((ND, SEG, F), BF),
            pltpu.VMEM((ND * SEG, F), F32),
            pltpu.VMEM((ROWS, F), F32),
            pltpu.VMEM((NB, BLK, F), BF),
            pltpu.VMEM((PER, F), I32),
            pltpu.SMEM((PER, F), I32),
            pltpu.SemaphoreType.DMA,
            pltpu.SemaphoreType.DMA,
            pltpu.SemaphoreType.DMA((PARTS,)),
            pltpu.SemaphoreType.DMA,
            pltpu.SemaphoreType.DMA,
        ],
        compiler_params=params(56),
        name="unpack",
    )(send_blocks, arrived)


def prepare_kernel(
    row_s, col_s, count_s, send_blocks, tile_vals, relaid,
    pairs, base, inv_out, lists,
    tiles, acc, held, cursor, tile_k, sem,
):
    load = pltpu.make_async_copy(tile_vals, tiles.at[pl.ds(0, TILES)], sem)
    load.start()
    tiles[TILES] = jnp.zeros((BLK, BLK), I32)
    acc[...] = jnp.zeros_like(acc)

    def clear(i, _):
        cursor[i] = 0
        return 0

    lax.fori_loop(0, 2 * NB, clear, 0)

    def clear_pair(i, _):
        lists[ROW + i] = 0
        for s in (0, 1):
            tile_k[2 * i + s] = TILES
            lists[COL + 2 * i + s] = 0
        return 0

    lax.fori_loop(0, PAIRS, clear_pair, 0)
    used = count_s[0]

    def tally(t, _):
        g = row_s[t] + jnp.where(col_s[t] >= NB, NB, 0)
        cursor[g] = cursor[g] + 1
        return 0

    lax.fori_loop(0, used, tally, 0)

    def starts(g, at):
        n = cursor[g]
        cursor[g] = 2 * at
        return at + ((n + 1) >> 1)

    n_own = lax.fori_loop(0, NB, starts, 0)
    n_own = (n_own + GROUP - 1) // GROUP * GROUP
    n_all = lax.fori_loop(NB, 2 * NB, starts, n_own)
    n_all = (n_all + GROUP - 1) // GROUP * GROUP
    lists[META + 0] = n_own
    lists[META + 1] = n_all

    def place(t, _):
        row = row_s[t]
        col = col_s[t]
        far = col >= NB
        col = jnp.where(far, col - NB, col)
        g = row + jnp.where(far, NB, 0)
        at = cursor[g]
        cursor[g] = at + 1
        tile_k[at] = t
        lists[COL + at] = col
        lists[ROW + at >> 1] = row
        return 0

    lax.fori_loop(0, used, place, 0)

    def zero_dest(i, _):
        cursor[i] = 0
        return 0

    lax.fori_loop(0, NB, zero_dest, 0)

    def tally_dest(d, _):
        b = send_blocks[d]
        cursor[b] = cursor[b] + 1
        return 0

    lax.fori_loop(0, ND, tally_dest, 0)

    def starts_dest(b, at):
        n = cursor[b]
        cursor[b] = at
        lists[DEST_AT + b] = at
        return at + n

    lists[DEST_AT + NB] = lax.fori_loop(0, NB, starts_dest, 0)

    def place_dest(d, _):
        b = send_blocks[d]
        at = cursor[b]
        cursor[b] = at + 1
        lists[DEST + at] = d
        return 0

    lax.fori_loop(0, ND, place_dest, 0)
    load.wait()
    ones = jnp.ones((2 * BLK, BLK), BF)

    def fetch(k):
        v = jnp.concatenate([tiles[tile_k[2 * k]], tiles[tile_k[2 * k + 1]]], axis=1)
        v = v.astype(F32).astype(BF)
        pairs[k] = v
        return v

    def own(i, _):
        for u in range(UNROLL):
            k = i * UNROLL + u
            v = fetch(k)
            x = jnp.concatenate([relaid[lists[COL + 2 * k]], relaid[lists[COL + 2 * k + 1]]], axis=0)
            got = mm(v, jnp.concatenate([x, ones], axis=1))
            acc[lists[ROW + k]] += got
        return 0

    lax.fori_loop(0, n_own // UNROLL, own, 0)

    def far(i, _):
        for u in range(UNROLL):
            k = i * UNROLL + u
            r = lists[ROW + k]
            acc[r, :, BLK:] += mm(fetch(k), ones)
        return 0

    lax.fori_loop(n_own // UNROLL, n_all // UNROLL, far, 0)
    inv = 1.0 / jnp.maximum(acc[:, :, BLK:], 1.0)
    inv_out[...] = inv
    base[...] = acc[:, :, :BLK] * inv


def prepare(tile_row, tile_col, tile_count, send_blocks, tile_vals, relaid):
    return pl.pallas_call(
        prepare_kernel,
        out_shape=(
            jax.ShapeDtypeStruct((PAIRS, BLK, 2 * BLK), BF),
            jax.ShapeDtypeStruct((NB, BLK, F), F32),
            jax.ShapeDtypeStruct((NB, BLK, BLK), F32),
            jax.ShapeDtypeStruct((LISTS,), I32),
        ),
        in_specs=[SMEM, SMEM, SMEM, SMEM, ANY, VMEM],
        out_specs=(VMEM, VMEM, VMEM, SMEM),
        scratch_shapes=[
            pltpu.VMEM((TILES + 1, BLK, BLK), I32),
            pltpu.VMEM((NB, BLK, 2 * BLK), F32),
            pltpu.VMEM((8, BLK), F32),
            pltpu.SMEM((2 * NB,), I32),
            pltpu.SMEM((2 * PAIRS,), I32),
            pltpu.SemaphoreType.DMA,
        ],
        compiler_params=params(56),
        cost_estimate=cost(2 * 10**9, 32 * 2**20),
        name="prepare",
    )(tile_row, tile_col, tile_count, send_blocks, tile_vals, relaid)


def load_pairs(first, last, pairs, held, sems, begin=0, end=PAIRS):
    def group(c, _):
        pltpu.make_async_copy(
            pairs.at[pl.ds(first + c * GROUP, GROUP)], held.at[pl.ds(c * GROUP, GROUP)], sems.at[c]
        ).start()
        return 0

    groups = (last - first) // GROUP
    lax.fori_loop(jnp.minimum(begin, groups), jnp.minimum(end, groups), group, 0)


def row_copies(i, base, inv, base_v, inv_v, sems_base, sems_inv):
    b = pl.ds(BATCH * i, BATCH)
    return (
        pltpu.make_async_copy(base.at[b], base_v.at[b], sems_base.at[i]),
        pltpu.make_async_copy(inv.at[b], inv_v.at[b], sems_inv.at[i]),
    )


def add_pairs(first, last, held, sems, table, acc, lists, finish):
    groups = (last - first) // GROUP

    def group(c, done):
        pltpu.make_async_copy(held.at[pl.ds(0, GROUP)], held.at[pl.ds(0, GROUP)], sems.at[c]).wait()
        for u0 in range(0, GROUP, UNROLL):
            for u in range(u0, u0 + UNROLL):
                k = first + c * GROUP + u
                x = jnp.concatenate([table[lists[COL + 2 * k]], table[lists[COL + 2 * k + 1]]], axis=0)
                got = mm(held[c * GROUP + u], x)
                acc[lists[ROW + k]] += got
        following = lists[ROW + jnp.minimum(first + (c + 1) * GROUP, PAIRS - 1)]
        upto = jnp.where(c + 1 < groups, following, NB) // BATCH
        lax.fori_loop(done, upto, finish, 0)
        return upto

    lax.fori_loop(lax.fori_loop(0, groups, group, 0), BATCHES, finish, 0)


def first_kernel(
    lists_in, remote, pairs, base, inv, mean_out, send,
    lists, table, held, base_v, inv_v, acc, mean, sems, sems_base, sems_inv, sem_lists, sem_table, sem_mean, sem_out,
):
    load_table = pltpu.make_async_copy(remote, table, sem_table)
    rows = lambda i: row_copies(i, base, inv, base_v, inv_v, sems_base, sems_inv)

    def load(i, _):
        load_pairs(lists[META + 0], lists[META + 1], pairs, held, sems, LOADS * i, LOADS * (i + 1))
        for copy in rows(i):
            copy.start()
        return 0

    load_lists = pltpu.make_async_copy(lists_in, lists, sem_lists)
    load_lists.start()
    load_table.start()
    load_lists.wait()
    lax.fori_loop(0, EARLY, load, 0)
    acc[...] = jnp.zeros_like(acc)
    load_table.wait()
    lax.fori_loop(EARLY, BATCHES, load, 0)
    load_pairs(lists[META + 0], lists[META + 1], pairs, held, sems, LOADS * BATCHES)

    def finish(i, _):
        for copy in rows(i):
            copy.wait()
        b = pl.ds(BATCH * i, BATCH)
        mean[b] = (base_v[b] + acc[b] * inv_v[b]).astype(BF)
        pltpu.make_async_copy(mean.at[b], mean_out.at[b], sem_mean).start()

        def post(j, blk):
            blk = lax.while_loop(lambda at: j >= lists[DEST_AT + at + 1], lambda at: at + 1, blk)
            pltpu.make_async_copy(mean.at[blk], send.at[lists[DEST + j]], sem_out).start()
            return blk

        lax.fori_loop(lists[DEST_AT + BATCH * i], lists[DEST_AT + BATCH * (i + 1)], post, BATCH * i)
        return 0

    add_pairs(lists[META + 0], lists[META + 1], held, sems, table, acc, lists, finish)
    pltpu.make_async_copy(mean_out, mean_out, sem_mean).wait()
    pltpu.make_async_copy(send, send, sem_out).wait()


def first(lists, pairs, remote, base, inv):
    return pl.pallas_call(
        first_kernel,
        out_shape=(
            jax.ShapeDtypeStruct((NB, BLK, F), BF),
            jax.ShapeDtypeStruct((ND, BLK, F), BF),
        ),
        in_specs=[ANY] * 5,
        out_specs=(ANY, ANY),
        scratch_shapes=[
            pltpu.SMEM((LISTS,), I32),
            pltpu.VMEM((ND, BLK, F), BF),
            pltpu.VMEM((PAIRS, BLK, 2 * BLK), BF),
            pltpu.VMEM((NB, BLK, F), F32),
            pltpu.VMEM((NB, BLK, BLK), F32),
            pltpu.VMEM((NB, BLK, F), F32),
            pltpu.VMEM((NB, BLK, F), BF),
            pltpu.SemaphoreType.DMA((PAIRS // GROUP,)),
            pltpu.SemaphoreType.DMA((BATCHES,)),
            pltpu.SemaphoreType.DMA((BATCHES,)),
        ]
        + [pltpu.SemaphoreType.DMA] * 4,
        compiler_params=params(56),
        name="first_layer",
    )(lists, remote, pairs, base, inv)


def own_kernel(
    lists, pairs, relaid, mean, inv, w_self1, w_neigh1, w_self2, w_neigh2, base,
    hidden, acc, held, sems,
):
    load_pairs(0, lists[META + 0], pairs, held, sems)
    acc[...] = jnp.zeros_like(acc)
    weights = jnp.concatenate([w_self1[...], w_neigh1[...]], axis=0)
    final = jnp.concatenate([w_self2[...], w_neigh2[...], w_neigh2[...]], axis=0)

    def layer(i, _):
        b = pl.ds(2 * i, 2)
        x = jnp.concatenate([relaid[b].reshape(2 * BLK, F), mean[b].reshape(2 * BLK, F)], axis=1)
        hidden[b] = jnp.maximum(mm(x, weights), 0.0).astype(BF).reshape(2, BLK, H)
        return 0

    lax.fori_loop(0, NB // 2, layer, 0)

    def finish(i, _):
        b = pl.ds(BATCH * i, BATCH)
        scale = inv[b].reshape(BATCH * BLK, BLK)
        m = acc[b].reshape(BATCH * BLK, H) * jnp.concatenate([scale, scale], axis=1)
        high = m.astype(BF)
        low = (m - high.astype(F32)).astype(BF)
        x = jnp.concatenate([hidden[b].reshape(BATCH * BLK, H), high, low], axis=1)
        base[b] = mm(x, final).reshape(BATCH, BLK, H)
        return 0

    add_pairs(0, lists[META + 0], held, sems, hidden, acc, lists, finish)


def own_part(lists, pairs, relaid, mean, inv, w_self1, w_neigh1, w_self2, w_neigh2):
    return pl.pallas_call(
        own_kernel,
        out_shape=jax.ShapeDtypeStruct((NB, BLK, H), F32),
        in_specs=[SMEM, ANY] + [VMEM] * 7,
        out_specs=VMEM,
        scratch_shapes=[
            pltpu.VMEM((NB, BLK, H), BF),
            pltpu.VMEM((NB, BLK, H), F32),
            pltpu.VMEM((PAIRS, BLK, 2 * BLK), BF),
            pltpu.SemaphoreType.DMA((PAIRS // GROUP,)),
        ],
        compiler_params=params(56),
        cost_estimate=cost(2 * 10**9, 32 * 2**20),
        name="own_part",
    )(lists, pairs, relaid, mean, inv, w_self1, w_neigh1, w_self2, w_neigh2)


EARLY = 2
LOADS = 2
CHUNK = ND // BATCHES


def second_kernel(
    lists, near, far, pairs, base, inv, w_self1, w_neigh1, w_neigh2, out,
    near_v, far_v, table, held, base_v, inv_v, acc, result,
    sems, sems_near, sems_far, sems_base, sems_inv, sem_out,
):
    def chunk(c):
        part = pl.ds(c * CHUNK, CHUNK)
        return (
            pltpu.make_async_copy(near.at[part], near_v.at[part], sems_near.at[c]),
            pltpu.make_async_copy(far.at[part], far_v.at[part], sems_far.at[c]),
        )

    rows = lambda i: row_copies(i, base, inv, base_v, inv_v, sems_base, sems_inv)

    def load(i):
        load_pairs(lists[META + 0], lists[META + 1], pairs, held, sems, LOADS * i, LOADS * (i + 1))
        for copy in rows(i):
            copy.start()

    for c in range(ND // CHUNK):
        for copy in chunk(c):
            copy.start()
    acc[...] = jnp.zeros_like(acc)
    weights = jnp.concatenate([w_self1[...], w_neigh1[...]], axis=0)

    def layer(c, _):
        for copy in chunk(c):
            copy.wait()
        load(c)
        for i in range(CHUNK // 2):
            b = pl.ds(c * CHUNK + 2 * i, 2)
            x = jnp.concatenate([near_v[b].reshape(2 * BLK, F), far_v[b].reshape(2 * BLK, F)], axis=1)
            table[b] = jnp.maximum(mm(x, weights), 0.0).astype(BF).reshape(2, BLK, H)
        return 0

    lax.fori_loop(0, BATCHES, layer, 0)
    load_pairs(lists[META + 0], lists[META + 1], pairs, held, sems, LOADS * BATCHES)

    def finish(i, _):
        for copy in rows(i):
            copy.wait()
        b = pl.ds(BATCH * i, BATCH)
        scale = inv_v[b].reshape(BATCH * BLK, BLK)
        m = acc[b].reshape(BATCH * BLK, H) * jnp.concatenate([scale, scale], axis=1)
        total = base_v[b].reshape(BATCH * BLK, H) + mm(m.astype(BF), w_neigh2[...])
        result[b] = total.astype(BF).reshape(BATCH, BLK, H)
        pltpu.make_async_copy(result.at[b], out.at[b], sem_out).start()
        return 0

    add_pairs(lists[META + 0], lists[META + 1], held, sems, table, acc, lists, finish)
    pltpu.make_async_copy(out, out, sem_out).wait()


def second(lists, near, far, pairs, base, inv, w_self1, w_neigh1, w_neigh2):
    return pl.pallas_call(
        second_kernel,
        out_shape=jax.ShapeDtypeStruct((NB, BLK, H), BF),
        in_specs=[SMEM] + [ANY] * 5 + [VMEM] * 3,
        out_specs=ANY,
        scratch_shapes=[
            pltpu.VMEM((ND, BLK, F), BF),
            pltpu.VMEM((ND, BLK, F), BF),
            pltpu.VMEM((ND, BLK, H), BF),
            pltpu.VMEM((PAIRS, BLK, 2 * BLK), BF),
            pltpu.VMEM((NB, BLK, H), F32),
            pltpu.VMEM((NB, BLK, BLK), F32),
            pltpu.VMEM((NB, BLK, H), F32),
            pltpu.VMEM((NB, BLK, H), BF),
            pltpu.SemaphoreType.DMA((PAIRS // GROUP,)),
        ]
        + [pltpu.SemaphoreType.DMA((BATCHES,))] * 4
        + [pltpu.SemaphoreType.DMA],
        compiler_params=params(56),
        name="second_layer",
    )(lists, near, far, pairs, base, inv, w_self1, w_neigh1, w_neigh2)


def exchange(x):
    return lax.all_to_all(x, "dom", split_axis=0, concat_axis=0, tiled=True)


def local(
    features, owner, slot, send_blocks, tile_row, tile_col, tile_vals, tile_count,
    w_self1, w_neigh1, w_self2, w_neigh2,
):
    picks = send_blocks.reshape(ND)
    arrived = exchange(pack(features, owner, slot))
    relaid, send = unpack(picks, arrived)
    near = exchange(send)
    pairs, base, inv, lists = prepare(tile_row, tile_col, tile_count, picks, tile_vals, relaid)
    mean, send = first(lists, pairs, near, base, inv)
    far = exchange(send)
    base = own_part(lists, pairs, relaid, mean, inv, w_self1, w_neigh1, w_self2, w_neigh2)
    return second(lists, near, far, pairs, base, inv, w_self1, w_neigh1, w_neigh2).reshape(ROWS, H)


def solution(mesh):
    rows, flat = P("dom", None), P("dom")
    cube = P("dom", None, None)
    placed = (rows, flat, flat, cube, flat, flat, cube, flat, P(), P(), P(), P())
    return jax.shard_map(local, mesh=mesh, in_specs=placed, out_specs=rows, check_vma=False)
```

```python
import jax
import jax.numpy as jnp
from jax import lax
from jax.experimental import pallas as pl
from jax.experimental.pallas import tpu as pltpu
from jax.sharding import PartitionSpec as P

F = 128
H = 256
BLK = 128
ROWS = 4096
TILES = 256
NB = 32
ND = 128
PER = ROWS // ND
SEG = PER + 8
PAIRS = 192
GROUP = 16
BATCH = 8
BATCHES = NB // BATCH
UNROLL = 4
ROW, COL, META, DEST, DEST_AT, LISTS = 0, PAIRS, 3 * PAIRS, 3 * PAIRS + 8, 3 * PAIRS + 136, 1024
BF = jnp.bfloat16
F32 = jnp.float32
I32 = jnp.int32

SMEM = pl.BlockSpec(memory_space=pltpu.SMEM)
VMEM = pl.BlockSpec(memory_space=pltpu.VMEM)
ANY = pl.BlockSpec(memory_space=pl.ANY)


def params(mib):
    return pltpu.CompilerParams(vmem_limit_bytes=mib * 1024 * 1024)


def cost(flops, nbytes):
    return pl.CostEstimate(flops=flops, bytes_accessed=nbytes, transcendentals=0)


def mm(a, b):
    return jnp.dot(a, b, preferred_element_type=F32)


def mm_t(a, b):
    return lax.dot_general(a, b, (((1,), (1,)), ((), ())), preferred_element_type=F32)


PARTS = 4


def pack_kernel(owner_in, slot_in, feat, out, rows, held, owner, slot, pos_v, pos_s, sems, sem_feat, sem_owner, sem_slot):
    load_owner = pltpu.make_async_copy(owner_in, owner, sem_owner)
    load_slot = pltpu.make_async_copy(slot_in, slot, sem_slot)
    load = pltpu.make_async_copy(feat, held, sem_feat)
    load_owner.start()
    load_slot.start()
    load.start()
    sub = lax.broadcasted_iota(I32, (BLK, BLK), 0)
    lane = lax.broadcasted_iota(I32, (BLK, BLK), 1)
    before = jnp.concatenate([(sub < lane).astype(BF), jnp.ones((BLK, BLK), BF)], axis=1)
    carry = jnp.zeros((BLK, BLK), F32)
    digits = jnp.zeros((BLK, BLK), F32)
    load_owner.wait()
    load_slot.wait()
    step = ROWS // BLK // PARTS

    def to_scalar(q):
        part = pl.ds(q * step, step)
        return pltpu.make_async_copy(pos_v.at[part], pos_s.at[part], sems.at[q])

    for c in range(ROWS // BLK):
        own = owner[c : c + 1, :]
        hit = own == sub
        hit_f = hit.astype(F32)
        counts = mm(hit_f.astype(BF), before)
        rank = jnp.sum(hit_f * (counts[:, :BLK] + carry), axis=0, keepdims=True)
        carry = carry + counts[:, BLK:]
        rank_i = rank.astype(I32)
        pos_v[c : c + 1, :] = own * SEG + rank_i
        places = slot[c : c + 1, :]
        high = (places >> 6).astype(F32)
        low = (places & 63).astype(F32)
        spread = jnp.concatenate([hit_f * high, hit_f * low], axis=1).astype(BF)
        ranks = jnp.concatenate([rank_i == sub, rank_i + PER == sub], axis=1).astype(F32).astype(BF)
        digits = digits + mm_t(spread, ranks)
        if c % step == step - 1:
            to_scalar(c // step).start()
    rows.reshape(ND, SEG, F)[:, PER:, :] = jnp.broadcast_to(digits[:, None, :], (ND, SEG - PER, F))
    load.wait()

    def move(c, _):
        for u in range(BLK):
            rows[pl.ds(pos_s[c, u], 1), :] = held[pl.ds(c * BLK + u, 1), :]
        return 0

    def moves(q, _):
        to_scalar(q).wait()
        return lax.fori_loop(q * step, (q + 1) * step, move, 0)

    lax.fori_loop(0, PARTS, moves, 0)
    out[...] = rows[...].reshape(ND, SEG, F).astype(BF)


def pack(features, owner, slot):
    return pl.pallas_call(
        pack_kernel,
        out_shape=pltpu.VMEM((ND, SEG, F), BF),
        in_specs=[ANY] * 3,
        out_specs=VMEM,
        scratch_shapes=[
            pltpu.VMEM((ND * SEG, F), F32),
            pltpu.VMEM((ROWS, F), F32),
            pltpu.VMEM((ROWS // BLK, BLK), I32),
            pltpu.VMEM((ROWS // BLK, BLK), I32),
            pltpu.VMEM((ROWS // BLK, BLK), I32),
            pltpu.SMEM((ROWS // BLK, BLK), I32),
            pltpu.SemaphoreType.DMA((PARTS,)),
        ]
        + [pltpu.SemaphoreType.DMA] * 3,
        compiler_params=params(56),
        name="pack",
    )(owner.reshape(ROWS // BLK, BLK), slot.reshape(ROWS // BLK, BLK), features)


def unpack_kernel(
    send_in, arrived, relaid_out, send,
    send_blocks, rows, placed, relaid, slot_v, slot_s, sem_send, sems, sem_relaid, sem_out,
):
    load_send = pltpu.make_async_copy(send_in, send_blocks, sem_send)
    load_send.start()
    senders = ND // PARTS
    step = senders * PER // F
    lane = lax.broadcasted_iota(I32, (step, F), 1)

    def to_scalar(q):
        part = pl.ds(q * step, step)
        return pltpu.make_async_copy(slot_v.at[part], slot_s.at[part], sems.at[q])

    for q in range(PARTS):
        size = senders * SEG
        rows[pl.ds(q * size, size), :] = arrived[pl.ds(q * senders, senders)].astype(F32).reshape(size, F)
        digits = rows[pl.ds(q * size + PER, senders, stride=SEG), :]
        slots = digits * 64.0 + pltpu.roll(digits, F - PER, 1)
        total = jnp.where(lane < PER, slots[:step], 0.0)
        for g in range(1, F // PER):
            total += pltpu.roll(jnp.where(lane < PER, slots[step * g : step * (g + 1)], 0.0), PER * g, 1)
        slot_v[pl.ds(q * step, step), :] = total.astype(I32)
        to_scalar(q).start()

    def moves(q, _):
        to_scalar(q).wait()

        def move(i, _):
            for u in range(F):
                source = (q * senders + i + step * (u // PER)) * SEG + u % PER
                placed[pl.ds(slot_s[q * step + i, u], 1), :] = rows[pl.ds(source, 1), :]
            return 0

        return lax.fori_loop(0, step, move, 0)

    lax.fori_loop(0, PARTS, moves, 0)
    relaid[...] = placed[...].reshape(NB, BLK, F).astype(BF)
    load_send.wait()

    def post(d, _):
        pltpu.make_async_copy(relaid.at[send_blocks[d]], send.at[d], sem_out).start()
        return 0

    lax.fori_loop(0, ND, post, 0)
    keep = pltpu.make_async_copy(relaid, relaid_out, sem_relaid)
    keep.start()
    pltpu.make_async_copy(send, send, sem_out).wait()
    keep.wait()


def unpack(send_blocks, arrived):
    return pl.pallas_call(
        unpack_kernel,
        out_shape=(
            pltpu.HBM((NB, BLK, F), BF),
            pltpu.HBM((ND, BLK, F), BF),
        ),
        in_specs=[ANY, VMEM],
        out_specs=(ANY, ANY),
        scratch_shapes=[
            pltpu.SMEM((ND,), I32),
            pltpu.VMEM((ND * SEG, F), F32),
            pltpu.VMEM((ROWS, F), F32),
            pltpu.VMEM((NB, BLK, F), BF),
            pltpu.VMEM((PER, F), I32),
            pltpu.SMEM((PER, F), I32),
            pltpu.SemaphoreType.DMA,
            pltpu.SemaphoreType.DMA((PARTS,)),
            pltpu.SemaphoreType.DMA,
            pltpu.SemaphoreType.DMA,
        ],
        compiler_params=params(56),
        name="unpack",
    )(send_blocks, arrived)


def prepare_kernel(
    row_s, col_s, count_s, send_blocks, tile_vals, relaid,
    pairs, base, inv_out, lists,
    tiles, acc, held, cursor, tile_k, sem,
):
    load = pltpu.make_async_copy(tile_vals, tiles.at[pl.ds(0, TILES)], sem)
    load.start()
    tiles[TILES] = jnp.zeros((BLK, BLK), I32)
    acc[...] = jnp.zeros_like(acc)

    def clear(i, _):
        cursor[i] = 0
        return 0

    lax.fori_loop(0, 2 * NB, clear, 0)

    def clear_pair(i, _):
        lists[ROW + i] = 0
        for s in (0, 1):
            tile_k[2 * i + s] = TILES
            lists[COL + 2 * i + s] = 0
        return 0

    lax.fori_loop(0, PAIRS, clear_pair, 0)
    used = count_s[0]

    def tally(t, _):
        g = row_s[t] + jnp.where(col_s[t] >= NB, NB, 0)
        cursor[g] = cursor[g] + 1
        return 0

    lax.fori_loop(0, used, tally, 0)

    def starts(g, at):
        n = cursor[g]
        cursor[g] = 2 * at
        return at + ((n + 1) >> 1)

    n_own = lax.fori_loop(0, NB, starts, 0)
    n_own = (n_own + GROUP - 1) // GROUP * GROUP
    n_all = lax.fori_loop(NB, 2 * NB, starts, n_own)
    n_all = (n_all + GROUP - 1) // GROUP * GROUP
    lists[META + 0] = n_own
    lists[META + 1] = n_all

    def place(t, _):
        row = row_s[t]
        col = col_s[t]
        far = col >= NB
        col = jnp.where(far, col - NB, col)
        g = row + jnp.where(far, NB, 0)
        at = cursor[g]
        cursor[g] = at + 1
        tile_k[at] = t
        lists[COL + at] = col
        lists[ROW + at >> 1] = row
        return 0

    lax.fori_loop(0, used, place, 0)

    def zero_dest(i, _):
        cursor[i] = 0
        return 0

    lax.fori_loop(0, NB, zero_dest, 0)

    def tally_dest(d, _):
        b = send_blocks[d]
        cursor[b] = cursor[b] + 1
        return 0

    lax.fori_loop(0, ND, tally_dest, 0)

    def starts_dest(b, at):
        n = cursor[b]
        cursor[b] = at
        lists[DEST_AT + b] = at
        return at + n

    lists[DEST_AT + NB] = lax.fori_loop(0, NB, starts_dest, 0)

    def place_dest(d, _):
        b = send_blocks[d]
        at = cursor[b]
        cursor[b] = at + 1
        lists[DEST + at] = d
        return 0

    lax.fori_loop(0, ND, place_dest, 0)
    load.wait()
    ones = jnp.ones((2 * BLK, BLK), BF)

    def fetch(k):
        v = jnp.concatenate([tiles[tile_k[2 * k]], tiles[tile_k[2 * k + 1]]], axis=1)
        v = v.astype(F32).astype(BF)
        pairs[k] = v
        return v

    def own(i, _):
        for u in range(UNROLL):
            k = i * UNROLL + u
            v = fetch(k)
            x = jnp.concatenate([relaid[lists[COL + 2 * k]], relaid[lists[COL + 2 * k + 1]]], axis=0)
            got = mm(v, jnp.concatenate([x, ones], axis=1))
            acc[lists[ROW + k]] += got
        return 0

    lax.fori_loop(0, n_own // UNROLL, own, 0)

    def far(i, _):
        for u in range(UNROLL):
            k = i * UNROLL + u
            r = lists[ROW + k]
            acc[r, :, BLK:] += mm(fetch(k), ones)
        return 0

    lax.fori_loop(n_own // UNROLL, n_all // UNROLL, far, 0)
    inv = 1.0 / jnp.maximum(acc[:, :, BLK:], 1.0)
    inv_out[...] = inv
    base[...] = acc[:, :, :BLK] * inv


def prepare(tile_row, tile_col, tile_count, send_blocks, tile_vals, relaid):
    return pl.pallas_call(
        prepare_kernel,
        out_shape=(
            jax.ShapeDtypeStruct((PAIRS, BLK, 2 * BLK), BF),
            jax.ShapeDtypeStruct((NB, BLK, F), F32),
            jax.ShapeDtypeStruct((NB, BLK, BLK), F32),
            jax.ShapeDtypeStruct((LISTS,), I32),
        ),
        in_specs=[SMEM, SMEM, SMEM, SMEM, ANY, VMEM],
        out_specs=(VMEM, VMEM, VMEM, SMEM),
        scratch_shapes=[
            pltpu.VMEM((TILES + 1, BLK, BLK), I32),
            pltpu.VMEM((NB, BLK, 2 * BLK), F32),
            pltpu.VMEM((8, BLK), F32),
            pltpu.SMEM((2 * NB,), I32),
            pltpu.SMEM((2 * PAIRS,), I32),
            pltpu.SemaphoreType.DMA,
        ],
        compiler_params=params(56),
        cost_estimate=cost(2 * 10**9, 32 * 2**20),
        name="prepare",
    )(tile_row, tile_col, tile_count, send_blocks, tile_vals, relaid)


def load_pairs(first, last, pairs, held, sems, begin=0, end=PAIRS):
    def group(c, _):
        pltpu.make_async_copy(
            pairs.at[pl.ds(first + c * GROUP, GROUP)], held.at[pl.ds(c * GROUP, GROUP)], sems.at[c]
        ).start()
        return 0

    groups = (last - first) // GROUP
    lax.fori_loop(jnp.minimum(begin, groups), jnp.minimum(end, groups), group, 0)


def row_copies(i, base, inv, base_v, inv_v, sems_base, sems_inv):
    b = pl.ds(BATCH * i, BATCH)
    return (
        pltpu.make_async_copy(base.at[b], base_v.at[b], sems_base.at[i]),
        pltpu.make_async_copy(inv.at[b], inv_v.at[b], sems_inv.at[i]),
    )


def add_pairs(first, last, held, sems, table, acc, lists, finish):
    groups = (last - first) // GROUP

    def group(c, done):
        pltpu.make_async_copy(held.at[pl.ds(0, GROUP)], held.at[pl.ds(0, GROUP)], sems.at[c]).wait()
        for u0 in range(0, GROUP, UNROLL):
            for u in range(u0, u0 + UNROLL):
                k = first + c * GROUP + u
                x = jnp.concatenate([table[lists[COL + 2 * k]], table[lists[COL + 2 * k + 1]]], axis=0)
                got = mm(held[c * GROUP + u], x)
                acc[lists[ROW + k]] += got
        following = lists[ROW + jnp.minimum(first + (c + 1) * GROUP, PAIRS - 1)]
        upto = jnp.where(c + 1 < groups, following, NB) // BATCH
        lax.fori_loop(done, upto, finish, 0)
        return upto

    lax.fori_loop(lax.fori_loop(0, groups, group, 0), BATCHES, finish, 0)


def first_kernel(
    lists_in, remote, pairs, base, inv, mean_out, send,
    lists, table, held, base_v, inv_v, acc, mean, sems, sems_base, sems_inv, sem_lists, sem_table, sem_mean, sem_out,
):
    load_table = pltpu.make_async_copy(remote, table, sem_table)
    rows = lambda i: row_copies(i, base, inv, base_v, inv_v, sems_base, sems_inv)

    def load(i, _):
        load_pairs(lists[META + 0], lists[META + 1], pairs, held, sems, LOADS * i, LOADS * (i + 1))
        for copy in rows(i):
            copy.start()
        return 0

    load_lists = pltpu.make_async_copy(lists_in, lists, sem_lists)
    load_lists.start()
    load_table.start()
    load_lists.wait()
    lax.fori_loop(0, EARLY, load, 0)
    acc[...] = jnp.zeros_like(acc)
    load_table.wait()
    lax.fori_loop(EARLY, BATCHES, load, 0)
    load_pairs(lists[META + 0], lists[META + 1], pairs, held, sems, LOADS * BATCHES)

    def finish(i, _):
        for copy in rows(i):
            copy.wait()
        b = pl.ds(BATCH * i, BATCH)
        mean[b] = (base_v[b] + acc[b] * inv_v[b]).astype(BF)
        pltpu.make_async_copy(mean.at[b], mean_out.at[b], sem_mean).start()

        def post(j, blk):
            blk = lax.while_loop(lambda at: j >= lists[DEST_AT + at + 1], lambda at: at + 1, blk)
            pltpu.make_async_copy(mean.at[blk], send.at[lists[DEST + j]], sem_out).start()
            return blk

        lax.fori_loop(lists[DEST_AT + BATCH * i], lists[DEST_AT + BATCH * (i + 1)], post, BATCH * i)
        return 0

    add_pairs(lists[META + 0], lists[META + 1], held, sems, table, acc, lists, finish)
    pltpu.make_async_copy(mean_out, mean_out, sem_mean).wait()
    pltpu.make_async_copy(send, send, sem_out).wait()


def first(lists, pairs, remote, base, inv):
    return pl.pallas_call(
        first_kernel,
        out_shape=(
            jax.ShapeDtypeStruct((NB, BLK, F), BF),
            jax.ShapeDtypeStruct((ND, BLK, F), BF),
        ),
        in_specs=[ANY] * 5,
        out_specs=(ANY, ANY),
        scratch_shapes=[
            pltpu.SMEM((LISTS,), I32),
            pltpu.VMEM((ND, BLK, F), BF),
            pltpu.VMEM((PAIRS, BLK, 2 * BLK), BF),
            pltpu.VMEM((NB, BLK, F), F32),
            pltpu.VMEM((NB, BLK, BLK), F32),
            pltpu.VMEM((NB, BLK, F), F32),
            pltpu.VMEM((NB, BLK, F), BF),
            pltpu.SemaphoreType.DMA((PAIRS // GROUP,)),
            pltpu.SemaphoreType.DMA((BATCHES,)),
            pltpu.SemaphoreType.DMA((BATCHES,)),
        ]
        + [pltpu.SemaphoreType.DMA] * 4,
        compiler_params=params(56),
        name="first_layer",
    )(lists, remote, pairs, base, inv)


def own_kernel(
    lists, pairs, relaid, mean, inv, w_self1, w_neigh1, w_self2, w_neigh2, base,
    hidden, acc, held, sems,
):
    load_pairs(0, lists[META + 0], pairs, held, sems)
    acc[...] = jnp.zeros_like(acc)
    weights = jnp.concatenate([w_self1[...], w_neigh1[...]], axis=0)
    final = jnp.concatenate([w_self2[...], w_neigh2[...], w_neigh2[...]], axis=0)

    def layer(i, _):
        b = pl.ds(2 * i, 2)
        x = jnp.concatenate([relaid[b].reshape(2 * BLK, F), mean[b].reshape(2 * BLK, F)], axis=1)
        hidden[b] = jnp.maximum(mm(x, weights), 0.0).astype(BF).reshape(2, BLK, H)
        return 0

    lax.fori_loop(0, NB // 2, layer, 0)

    def finish(i, _):
        b = pl.ds(BATCH * i, BATCH)
        scale = inv[b].reshape(BATCH * BLK, BLK)
        m = acc[b].reshape(BATCH * BLK, H) * jnp.concatenate([scale, scale], axis=1)
        high = m.astype(BF)
        low = (m - high.astype(F32)).astype(BF)
        x = jnp.concatenate([hidden[b].reshape(BATCH * BLK, H), high, low], axis=1)
        base[b] = mm(x, final).reshape(BATCH, BLK, H)
        return 0

    add_pairs(0, lists[META + 0], held, sems, hidden, acc, lists, finish)


def own_part(lists, pairs, relaid, mean, inv, w_self1, w_neigh1, w_self2, w_neigh2):
    return pl.pallas_call(
        own_kernel,
        out_shape=jax.ShapeDtypeStruct((NB, BLK, H), F32),
        in_specs=[SMEM, ANY] + [VMEM] * 7,
        out_specs=VMEM,
        scratch_shapes=[
            pltpu.VMEM((NB, BLK, H), BF),
            pltpu.VMEM((NB, BLK, H), F32),
            pltpu.VMEM((PAIRS, BLK, 2 * BLK), BF),
            pltpu.SemaphoreType.DMA((PAIRS // GROUP,)),
        ],
        compiler_params=params(56),
        cost_estimate=cost(2 * 10**9, 32 * 2**20),
        name="own_part",
    )(lists, pairs, relaid, mean, inv, w_self1, w_neigh1, w_self2, w_neigh2)


EARLY = 2
LOADS = 2
CHUNK = ND // BATCHES


def second_kernel(
    lists, near, far, pairs, base, inv, w_self1, w_neigh1, w_neigh2, out,
    near_v, far_v, table, held, base_v, inv_v, acc, result,
    sems, sems_near, sems_far, sems_base, sems_inv, sem_out,
):
    def chunk(c):
        part = pl.ds(c * CHUNK, CHUNK)
        return (
            pltpu.make_async_copy(near.at[part], near_v.at[part], sems_near.at[c]),
            pltpu.make_async_copy(far.at[part], far_v.at[part], sems_far.at[c]),
        )

    rows = lambda i: row_copies(i, base, inv, base_v, inv_v, sems_base, sems_inv)

    def load(i):
        load_pairs(lists[META + 0], lists[META + 1], pairs, held, sems, LOADS * i, LOADS * (i + 1))
        for copy in rows(i):
            copy.start()

    for c in range(ND // CHUNK):
        for copy in chunk(c):
            copy.start()
    acc[...] = jnp.zeros_like(acc)
    weights = jnp.concatenate([w_self1[...], w_neigh1[...]], axis=0)

    def layer(c, _):
        for copy in chunk(c):
            copy.wait()
        load(c)
        for i in range(CHUNK // 2):
            b = pl.ds(c * CHUNK + 2 * i, 2)
            x = jnp.concatenate([near_v[b].reshape(2 * BLK, F), far_v[b].reshape(2 * BLK, F)], axis=1)
            table[b] = jnp.maximum(mm(x, weights), 0.0).astype(BF).reshape(2, BLK, H)
        return 0

    lax.fori_loop(0, BATCHES, layer, 0)
    load_pairs(lists[META + 0], lists[META + 1], pairs, held, sems, LOADS * BATCHES)

    def finish(i, _):
        for copy in rows(i):
            copy.wait()
        b = pl.ds(BATCH * i, BATCH)
        scale = inv_v[b].reshape(BATCH * BLK, BLK)
        m = acc[b].reshape(BATCH * BLK, H) * jnp.concatenate([scale, scale], axis=1)
        total = base_v[b].reshape(BATCH * BLK, H) + mm(m.astype(BF), w_neigh2[...])
        result[b] = total.astype(BF).reshape(BATCH, BLK, H)
        pltpu.make_async_copy(result.at[b], out.at[b], sem_out).start()
        return 0

    add_pairs(lists[META + 0], lists[META + 1], held, sems, table, acc, lists, finish)
    pltpu.make_async_copy(out, out, sem_out).wait()


def second(lists, near, far, pairs, base, inv, w_self1, w_neigh1, w_neigh2):
    return pl.pallas_call(
        second_kernel,
        out_shape=jax.ShapeDtypeStruct((NB, BLK, H), BF),
        in_specs=[SMEM] + [ANY] * 5 + [VMEM] * 3,
        out_specs=ANY,
        scratch_shapes=[
            pltpu.VMEM((ND, BLK, F), BF),
            pltpu.VMEM((ND, BLK, F), BF),
            pltpu.VMEM((ND, BLK, H), BF),
            pltpu.VMEM((PAIRS, BLK, 2 * BLK), BF),
            pltpu.VMEM((NB, BLK, H), F32),
            pltpu.VMEM((NB, BLK, BLK), F32),
            pltpu.VMEM((NB, BLK, H), F32),
            pltpu.VMEM((NB, BLK, H), BF),
            pltpu.SemaphoreType.DMA((PAIRS // GROUP,)),
        ]
        + [pltpu.SemaphoreType.DMA((BATCHES,))] * 4
        + [pltpu.SemaphoreType.DMA],
        compiler_params=params(56),
        name="second_layer",
    )(lists, near, far, pairs, base, inv, w_self1, w_neigh1, w_neigh2)


def exchange(x):
    return lax.all_to_all(x, "dom", split_axis=0, concat_axis=0, tiled=True)


def local(
    features, owner, slot, send_blocks, tile_row, tile_col, tile_vals, tile_count,
    w_self1, w_neigh1, w_self2, w_neigh2,
):
    picks = send_blocks.reshape(ND)
    features = pltpu.with_memory_space_constraint(features, pltpu.HBM)
    arrived = pltpu.with_memory_space_constraint(exchange(pack(features, owner, slot)), pltpu.VMEM)
    relaid, send = unpack(picks, arrived)
    near = exchange(send)
    pairs, base, inv, lists = prepare(tile_row, tile_col, tile_count, picks, tile_vals, relaid)
    mean, send = first(lists, pairs, near, base, inv)
    far = exchange(send)
    base = own_part(lists, pairs, relaid, mean, inv, w_self1, w_neigh1, w_self2, w_neigh2)
    return second(lists, near, far, pairs, base, inv, w_self1, w_neigh1, w_neigh2).reshape(ROWS, H)


def solution(mesh):
    rows, flat = P("dom", None), P("dom")
    cube = P("dom", None, None)
    placed = (rows, flat, flat, cube, flat, flat, cube, flat, P(), P(), P(), P())
    return jax.shard_map(local, mesh=mesh, in_specs=placed, out_specs=rows, check_vma=False)
```

```python
import jax
import jax.numpy as jnp
from jax import lax
from jax.experimental import pallas as pl
from jax.experimental.pallas import tpu as pltpu
from jax.sharding import PartitionSpec as P

F = 128
H = 256
BLK = 128
ROWS = 4096
TILES = 256
NB = 32
ND = 128
PER = ROWS // ND
SEG = PER + 2
PAIRS = 192
GROUP = 16
BATCH = 8
BATCHES = NB // BATCH
UNROLL = 4
ROW, COL, META, DEST, DEST_AT, LISTS = 0, PAIRS, 3 * PAIRS, 3 * PAIRS + 8, 3 * PAIRS + 136, 1024
BF = jnp.bfloat16
F32 = jnp.float32
I32 = jnp.int32

SMEM = pl.BlockSpec(memory_space=pltpu.SMEM)
VMEM = pl.BlockSpec(memory_space=pltpu.VMEM)
ANY = pl.BlockSpec(memory_space=pl.ANY)


def params(mib):
    return pltpu.CompilerParams(vmem_limit_bytes=mib * 1024 * 1024)


def cost(flops, nbytes):
    return pl.CostEstimate(flops=flops, bytes_accessed=nbytes, transcendentals=0)


def mm(a, b):
    return jnp.dot(a, b, preferred_element_type=F32)


def mm_t(a, b):
    return lax.dot_general(a, b, (((1,), (1,)), ((), ())), preferred_element_type=F32)


PARTS = 4


def pack_kernel(owner_in, slot_in, feat, out, rows, held, owner, slot, pos_v, pos_s, sems, sem_feat, sem_owner, sem_slot):
    load_owner = pltpu.make_async_copy(owner_in, owner, sem_owner)
    load_slot = pltpu.make_async_copy(slot_in, slot, sem_slot)
    load = pltpu.make_async_copy(feat, held, sem_feat)
    load_owner.start()
    load_slot.start()
    load.start()
    sub = lax.broadcasted_iota(I32, (BLK, BLK), 0)
    lane = lax.broadcasted_iota(I32, (BLK, BLK), 1)
    before = jnp.concatenate([(sub < lane).astype(BF), jnp.ones((BLK, BLK), BF)], axis=1)
    carry = jnp.zeros((BLK, BLK), F32)
    digits = jnp.zeros((BLK, BLK), F32)
    load_owner.wait()
    load_slot.wait()
    step = ROWS // BLK // PARTS

    def to_scalar(q):
        part = pl.ds(q * step, step)
        return pltpu.make_async_copy(pos_v.at[part], pos_s.at[part], sems.at[q])

    for c in range(ROWS // BLK):
        own = owner[c : c + 1, :]
        hit = own == sub
        hit_f = hit.astype(F32)
        counts = mm(hit_f.astype(BF), before)
        rank = jnp.sum(hit_f * (counts[:, :BLK] + carry), axis=0, keepdims=True)
        carry = carry + counts[:, BLK:]
        rank_i = rank.astype(I32)
        pos_v[c : c + 1, :] = own * SEG + rank_i
        places = slot[c : c + 1, :]
        high = (places >> 6).astype(F32)
        low = (places & 63).astype(F32)
        spread = jnp.concatenate([hit_f * high, hit_f * low], axis=1).astype(BF)
        ranks = jnp.concatenate([rank_i == sub, rank_i + PER == sub], axis=1).astype(F32).astype(BF)
        digits = digits + mm_t(spread, ranks)
        if c % step == step - 1:
            to_scalar(c // step).start()
    for extra in range(PER, SEG):
        rows[pl.ds(extra, ND, stride=SEG), :] = digits
    load.wait()

    def move(c, _):
        for u in range(BLK):
            rows[pl.ds(pos_s[c, u], 1), :] = held[pl.ds(c * BLK + u, 1), :]
        return 0

    def moves(q, _):
        to_scalar(q).wait()
        return lax.fori_loop(q * step, (q + 1) * step, move, 0)

    lax.fori_loop(0, PARTS, moves, 0)
    out[...] = rows[...].astype(BF)


def pack(features, owner, slot):
    return pl.pallas_call(
        pack_kernel,
        out_shape=pltpu.VMEM((ND * SEG, F), BF),
        in_specs=[ANY] * 3,
        out_specs=VMEM,
        scratch_shapes=[
            pltpu.VMEM((ND * SEG, F), F32),
            pltpu.VMEM((ROWS, F), F32),
            pltpu.VMEM((ROWS // BLK, BLK), I32),
            pltpu.VMEM((ROWS // BLK, BLK), I32),
            pltpu.VMEM((ROWS // BLK, BLK), I32),
            pltpu.SMEM((ROWS // BLK, BLK), I32),
            pltpu.SemaphoreType.DMA((PARTS,)),
        ]
        + [pltpu.SemaphoreType.DMA] * 3,
        compiler_params=params(56),
        name="pack",
    )(owner.reshape(ROWS // BLK, BLK), slot.reshape(ROWS // BLK, BLK), features)


def unpack_kernel(
    send_in, arrived, relaid_out, send,
    send_blocks, rows, placed, relaid, slot_v, slot_s, sem_send, sems, sem_relaid, sem_out,
):
    load_send = pltpu.make_async_copy(send_in, send_blocks, sem_send)
    load_send.start()
    senders = ND // PARTS
    step = senders * PER // F
    lane = lax.broadcasted_iota(I32, (step, F), 1)

    def to_scalar(q):
        part = pl.ds(q * step, step)
        return pltpu.make_async_copy(slot_v.at[part], slot_s.at[part], sems.at[q])

    for q in range(PARTS):
        size = senders * SEG
        rows[pl.ds(q * size, size), :] = arrived[pl.ds(q * size, size), :].astype(F32)
        digits = rows[pl.ds(q * size + PER, senders, stride=SEG), :]
        slots = digits * 64.0 + pltpu.roll(digits, F - PER, 1)
        total = jnp.where(lane < PER, slots[:step], 0.0)
        for g in range(1, F // PER):
            total += pltpu.roll(jnp.where(lane < PER, slots[step * g : step * (g + 1)], 0.0), PER * g, 1)
        slot_v[pl.ds(q * step, step), :] = total.astype(I32)
        to_scalar(q).start()

    def moves(q, _):
        to_scalar(q).wait()

        def move(i, _):
            for u in range(F):
                source = (q * senders + i + step * (u // PER)) * SEG + u % PER
                placed[pl.ds(slot_s[q * step + i, u], 1), :] = rows[pl.ds(source, 1), :]
            return 0

        return lax.fori_loop(0, step, move, 0)

    lax.fori_loop(0, PARTS, moves, 0)
    relaid[...] = placed[...].reshape(NB, BLK, F).astype(BF)
    load_send.wait()

    def post(d, _):
        pltpu.make_async_copy(relaid.at[send_blocks[d]], send.at[d], sem_out).start()
        return 0

    lax.fori_loop(0, ND, post, 0)
    keep = pltpu.make_async_copy(relaid, relaid_out, sem_relaid)
    keep.start()
    pltpu.make_async_copy(send, send, sem_out).wait()
    keep.wait()


def unpack(send_blocks, arrived):
    return pl.pallas_call(
        unpack_kernel,
        out_shape=(
            pltpu.HBM((NB, BLK, F), BF),
            pltpu.HBM((ND, BLK, F), BF),
        ),
        in_specs=[ANY, VMEM],
        out_specs=(ANY, ANY),
        scratch_shapes=[
            pltpu.SMEM((ND,), I32),
            pltpu.VMEM((ND * SEG, F), F32),
            pltpu.VMEM((ROWS, F), F32),
            pltpu.VMEM((NB, BLK, F), BF),
            pltpu.VMEM((PER, F), I32),
            pltpu.SMEM((PER, F), I32),
            pltpu.SemaphoreType.DMA,
            pltpu.SemaphoreType.DMA((PARTS,)),
            pltpu.SemaphoreType.DMA,
            pltpu.SemaphoreType.DMA,
        ],
        compiler_params=params(56),
        name="unpack",
    )(send_blocks, arrived)


def prepare_kernel(
    row_s, col_s, count_s, send_blocks, tile_vals, relaid,
    pairs, base, inv_out, lists,
    tiles, acc, held, cursor, tile_k, sem,
):
    load = pltpu.make_async_copy(tile_vals, tiles.at[pl.ds(0, TILES)], sem)
    load.start()
    tiles[TILES] = jnp.zeros((BLK, BLK), I32)
    acc[...] = jnp.zeros_like(acc)

    def clear(i, _):
        cursor[i] = 0
        return 0

    lax.fori_loop(0, 2 * NB, clear, 0)

    def clear_pair(i, _):
        lists[ROW + i] = 0
        for s in (0, 1):
            tile_k[2 * i + s] = TILES
            lists[COL + 2 * i + s] = 0
        return 0

    lax.fori_loop(0, PAIRS, clear_pair, 0)
    used = count_s[0]

    def tally(t, _):
        g = row_s[t] + jnp.where(col_s[t] >= NB, NB, 0)
        cursor[g] = cursor[g] + 1
        return 0

    lax.fori_loop(0, used, tally, 0)

    def starts(g, at):
        n = cursor[g]
        cursor[g] = 2 * at
        return at + ((n + 1) >> 1)

    n_own = lax.fori_loop(0, NB, starts, 0)
    n_own = (n_own + GROUP - 1) // GROUP * GROUP
    n_all = lax.fori_loop(NB, 2 * NB, starts, n_own)
    n_all = (n_all + GROUP - 1) // GROUP * GROUP
    lists[META + 0] = n_own
    lists[META + 1] = n_all

    def place(t, _):
        row = row_s[t]
        col = col_s[t]
        far = col >= NB
        col = jnp.where(far, col - NB, col)
        g = row + jnp.where(far, NB, 0)
        at = cursor[g]
        cursor[g] = at + 1
        tile_k[at] = t
        lists[COL + at] = col
        lists[ROW + at >> 1] = row
        return 0

    lax.fori_loop(0, used, place, 0)

    def zero_dest(i, _):
        cursor[i] = 0
        return 0

    lax.fori_loop(0, NB, zero_dest, 0)

    def tally_dest(d, _):
        b = send_blocks[d]
        cursor[b] = cursor[b] + 1
        return 0

    lax.fori_loop(0, ND, tally_dest, 0)

    def starts_dest(b, at):
        n = cursor[b]
        cursor[b] = at
        lists[DEST_AT + b] = at
        return at + n

    lists[DEST_AT + NB] = lax.fori_loop(0, NB, starts_dest, 0)

    def place_dest(d, _):
        b = send_blocks[d]
        at = cursor[b]
        cursor[b] = at + 1
        lists[DEST + at] = d
        return 0

    lax.fori_loop(0, ND, place_dest, 0)
    load.wait()
    ones = jnp.ones((2 * BLK, BLK), BF)

    def fetch(k):
        v = jnp.concatenate([tiles[tile_k[2 * k]], tiles[tile_k[2 * k + 1]]], axis=1)
        v = v.astype(F32).astype(BF)
        pairs[k] = v
        return v

    def own(i, _):
        for u in range(UNROLL):
            k = i * UNROLL + u
            v = fetch(k)
            x = jnp.concatenate([relaid[lists[COL + 2 * k]], relaid[lists[COL + 2 * k + 1]]], axis=0)
            got = mm(v, jnp.concatenate([x, ones], axis=1))
            acc[lists[ROW + k]] += got
        return 0

    lax.fori_loop(0, n_own // UNROLL, own, 0)

    def far(i, _):
        for u in range(UNROLL):
            k = i * UNROLL + u
            r = lists[ROW + k]
            acc[r, :, BLK:] += mm(fetch(k), ones)
        return 0

    lax.fori_loop(n_own // UNROLL, n_all // UNROLL, far, 0)
    inv = 1.0 / jnp.maximum(acc[:, :, BLK:], 1.0)
    inv_out[...] = inv
    base[...] = acc[:, :, :BLK] * inv


def prepare(tile_row, tile_col, tile_count, send_blocks, tile_vals, relaid):
    return pl.pallas_call(
        prepare_kernel,
        out_shape=(
            jax.ShapeDtypeStruct((PAIRS, BLK, 2 * BLK), BF),
            jax.ShapeDtypeStruct((NB, BLK, F), F32),
            jax.ShapeDtypeStruct((NB, BLK, BLK), F32),
            jax.ShapeDtypeStruct((LISTS,), I32),
        ),
        in_specs=[SMEM, SMEM, SMEM, SMEM, ANY, VMEM],
        out_specs=(VMEM, VMEM, VMEM, SMEM),
        scratch_shapes=[
            pltpu.VMEM((TILES + 1, BLK, BLK), I32),
            pltpu.VMEM((NB, BLK, 2 * BLK), F32),
            pltpu.VMEM((8, BLK), F32),
            pltpu.SMEM((2 * NB,), I32),
            pltpu.SMEM((2 * PAIRS,), I32),
            pltpu.SemaphoreType.DMA,
        ],
        compiler_params=params(56),
        cost_estimate=cost(2 * 10**9, 32 * 2**20),
        name="prepare",
    )(tile_row, tile_col, tile_count, send_blocks, tile_vals, relaid)


def load_pairs(first, last, pairs, held, sems, begin=0, end=PAIRS):
    def group(c, _):
        pltpu.make_async_copy(
            pairs.at[pl.ds(first + c * GROUP, GROUP)], held.at[pl.ds(c * GROUP, GROUP)], sems.at[c]
        ).start()
        return 0

    groups = (last - first) // GROUP
    lax.fori_loop(jnp.minimum(begin, groups), jnp.minimum(end, groups), group, 0)


def row_copies(i, base, inv, base_v, inv_v, sems_base, sems_inv):
    b = pl.ds(BATCH * i, BATCH)
    return (
        pltpu.make_async_copy(base.at[b], base_v.at[b], sems_base.at[i]),
        pltpu.make_async_copy(inv.at[b], inv_v.at[b], sems_inv.at[i]),
    )


def add_pairs(first, last, held, sems, table, acc, lists, finish):
    groups = (last - first) // GROUP

    def group(c, done):
        pltpu.make_async_copy(held.at[pl.ds(0, GROUP)], held.at[pl.ds(0, GROUP)], sems.at[c]).wait()
        for u0 in range(0, GROUP, UNROLL):
            for u in range(u0, u0 + UNROLL):
                k = first + c * GROUP + u
                x = jnp.concatenate([table[lists[COL + 2 * k]], table[lists[COL + 2 * k + 1]]], axis=0)
                got = mm(held[c * GROUP + u], x)
                acc[lists[ROW + k]] += got
        following = lists[ROW + jnp.minimum(first + (c + 1) * GROUP, PAIRS - 1)]
        upto = jnp.where(c + 1 < groups, following, NB) // BATCH
        lax.fori_loop(done, upto, finish, 0)
        return upto

    lax.fori_loop(lax.fori_loop(0, groups, group, 0), BATCHES, finish, 0)


def first_kernel(
    lists_in, remote, pairs, base, inv, mean_out, send,
    lists, table, held, base_v, inv_v, acc, mean, sems, sems_base, sems_inv, sem_lists, sem_table, sem_mean, sem_out,
):
    load_table = pltpu.make_async_copy(remote, table, sem_table)
    rows = lambda i: row_copies(i, base, inv, base_v, inv_v, sems_base, sems_inv)

    def load(i, _):
        load_pairs(lists[META + 0], lists[META + 1], pairs, held, sems, LOADS * i, LOADS * (i + 1))
        for copy in rows(i):
            copy.start()
        return 0

    load_lists = pltpu.make_async_copy(lists_in, lists, sem_lists)
    load_lists.start()
    load_table.start()
    load_lists.wait()
    lax.fori_loop(0, EARLY, load, 0)
    acc[...] = jnp.zeros_like(acc)
    load_table.wait()
    lax.fori_loop(EARLY, BATCHES, load, 0)
    load_pairs(lists[META + 0], lists[META + 1], pairs, held, sems, LOADS * BATCHES)

    def finish(i, _):
        for copy in rows(i):
            copy.wait()
        b = pl.ds(BATCH * i, BATCH)
        mean[b] = (base_v[b] + acc[b] * inv_v[b]).astype(BF)
        pltpu.make_async_copy(mean.at[b], mean_out.at[b], sem_mean).start()

        def post(j, blk):
            blk = lax.while_loop(lambda at: j >= lists[DEST_AT + at + 1], lambda at: at + 1, blk)
            pltpu.make_async_copy(mean.at[blk], send.at[lists[DEST + j]], sem_out).start()
            return blk

        lax.fori_loop(lists[DEST_AT + BATCH * i], lists[DEST_AT + BATCH * (i + 1)], post, BATCH * i)
        return 0

    add_pairs(lists[META + 0], lists[META + 1], held, sems, table, acc, lists, finish)
    pltpu.make_async_copy(mean_out, mean_out, sem_mean).wait()
    pltpu.make_async_copy(send, send, sem_out).wait()


def first(lists, pairs, remote, base, inv):
    return pl.pallas_call(
        first_kernel,
        out_shape=(
            jax.ShapeDtypeStruct((NB, BLK, F), BF),
            jax.ShapeDtypeStruct((ND, BLK, F), BF),
        ),
        in_specs=[ANY] * 5,
        out_specs=(ANY, ANY),
        scratch_shapes=[
            pltpu.SMEM((LISTS,), I32),
            pltpu.VMEM((ND, BLK, F), BF),
            pltpu.VMEM((PAIRS, BLK, 2 * BLK), BF),
            pltpu.VMEM((NB, BLK, F), F32),
            pltpu.VMEM((NB, BLK, BLK), F32),
            pltpu.VMEM((NB, BLK, F), F32),
            pltpu.VMEM((NB, BLK, F), BF),
            pltpu.SemaphoreType.DMA((PAIRS // GROUP,)),
            pltpu.SemaphoreType.DMA((BATCHES,)),
            pltpu.SemaphoreType.DMA((BATCHES,)),
        ]
        + [pltpu.SemaphoreType.DMA] * 4,
        compiler_params=params(56),
        name="first_layer",
    )(lists, remote, pairs, base, inv)


def own_kernel(
    lists, pairs, relaid, mean, inv, w_self1, w_neigh1, w_self2, w_neigh2, base,
    hidden, acc, held, sems,
):
    load_pairs(0, lists[META + 0], pairs, held, sems)
    acc[...] = jnp.zeros_like(acc)
    weights = jnp.concatenate([w_self1[...], w_neigh1[...]], axis=0)
    final = jnp.concatenate([w_self2[...], w_neigh2[...], w_neigh2[...]], axis=0)

    def layer(i, _):
        b = pl.ds(2 * i, 2)
        x = jnp.concatenate([relaid[b].reshape(2 * BLK, F), mean[b].reshape(2 * BLK, F)], axis=1)
        hidden[b] = jnp.maximum(mm(x, weights), 0.0).astype(BF).reshape(2, BLK, H)
        return 0

    lax.fori_loop(0, NB // 2, layer, 0)

    def finish(i, _):
        b = pl.ds(BATCH * i, BATCH)
        scale = inv[b].reshape(BATCH * BLK, BLK)
        m = acc[b].reshape(BATCH * BLK, H) * jnp.concatenate([scale, scale], axis=1)
        high = m.astype(BF)
        low = (m - high.astype(F32)).astype(BF)
        x = jnp.concatenate([hidden[b].reshape(BATCH * BLK, H), high, low], axis=1)
        base[b] = mm(x, final).reshape(BATCH, BLK, H)
        return 0

    add_pairs(0, lists[META + 0], held, sems, hidden, acc, lists, finish)


def own_part(lists, pairs, relaid, mean, inv, w_self1, w_neigh1, w_self2, w_neigh2):
    return pl.pallas_call(
        own_kernel,
        out_shape=jax.ShapeDtypeStruct((NB, BLK, H), F32),
        in_specs=[SMEM, ANY] + [VMEM] * 7,
        out_specs=VMEM,
        scratch_shapes=[
            pltpu.VMEM((NB, BLK, H), BF),
            pltpu.VMEM((NB, BLK, H), F32),
            pltpu.VMEM((PAIRS, BLK, 2 * BLK), BF),
            pltpu.SemaphoreType.DMA((PAIRS // GROUP,)),
        ],
        compiler_params=params(56),
        cost_estimate=cost(2 * 10**9, 32 * 2**20),
        name="own_part",
    )(lists, pairs, relaid, mean, inv, w_self1, w_neigh1, w_self2, w_neigh2)


EARLY = 2
LOADS = 2
CHUNK = ND // BATCHES


def second_kernel(
    lists, near, far, pairs, base, inv, w_self1, w_neigh1, w_neigh2, out,
    near_v, far_v, table, held, base_v, inv_v, acc, result,
    sems, sems_near, sems_far, sems_base, sems_inv, sem_out,
):
    def chunk(c):
        part = pl.ds(c * CHUNK, CHUNK)
        return (
            pltpu.make_async_copy(near.at[part], near_v.at[part], sems_near.at[c]),
            pltpu.make_async_copy(far.at[part], far_v.at[part], sems_far.at[c]),
        )

    rows = lambda i: row_copies(i, base, inv, base_v, inv_v, sems_base, sems_inv)

    def load(i):
        load_pairs(lists[META + 0], lists[META + 1], pairs, held, sems, LOADS * i, LOADS * (i + 1))
        for copy in rows(i):
            copy.start()

    for c in range(ND // CHUNK):
        for copy in chunk(c):
            copy.start()
    acc[...] = jnp.zeros_like(acc)
    weights = jnp.concatenate([w_self1[...], w_neigh1[...]], axis=0)

    def layer(c, _):
        for copy in chunk(c):
            copy.wait()
        load(c)
        for i in range(CHUNK // 2):
            b = pl.ds(c * CHUNK + 2 * i, 2)
            x = jnp.concatenate([near_v[b].reshape(2 * BLK, F), far_v[b].reshape(2 * BLK, F)], axis=1)
            table[b] = jnp.maximum(mm(x, weights), 0.0).astype(BF).reshape(2, BLK, H)
        return 0

    lax.fori_loop(0, BATCHES, layer, 0)
    load_pairs(lists[META + 0], lists[META + 1], pairs, held, sems, LOADS * BATCHES)

    def finish(i, _):
        for copy in rows(i):
            copy.wait()
        b = pl.ds(BATCH * i, BATCH)
        scale = inv_v[b].reshape(BATCH * BLK, BLK)
        m = acc[b].reshape(BATCH * BLK, H) * jnp.concatenate([scale, scale], axis=1)
        total = base_v[b].reshape(BATCH * BLK, H) + mm(m.astype(BF), w_neigh2[...])
        result[b] = total.astype(BF).reshape(BATCH, BLK, H)
        pltpu.make_async_copy(result.at[b], out.at[b], sem_out).start()
        return 0

    add_pairs(lists[META + 0], lists[META + 1], held, sems, table, acc, lists, finish)
    pltpu.make_async_copy(out, out, sem_out).wait()


def second(lists, near, far, pairs, base, inv, w_self1, w_neigh1, w_neigh2):
    return pl.pallas_call(
        second_kernel,
        out_shape=jax.ShapeDtypeStruct((NB, BLK, H), BF),
        in_specs=[SMEM] + [ANY] * 5 + [VMEM] * 3,
        out_specs=ANY,
        scratch_shapes=[
            pltpu.VMEM((ND, BLK, F), BF),
            pltpu.VMEM((ND, BLK, F), BF),
            pltpu.VMEM((ND, BLK, H), BF),
            pltpu.VMEM((PAIRS, BLK, 2 * BLK), BF),
            pltpu.VMEM((NB, BLK, H), F32),
            pltpu.VMEM((NB, BLK, BLK), F32),
            pltpu.VMEM((NB, BLK, H), F32),
            pltpu.VMEM((NB, BLK, H), BF),
            pltpu.SemaphoreType.DMA((PAIRS // GROUP,)),
        ]
        + [pltpu.SemaphoreType.DMA((BATCHES,))] * 4
        + [pltpu.SemaphoreType.DMA],
        compiler_params=params(56),
        name="second_layer",
    )(lists, near, far, pairs, base, inv, w_self1, w_neigh1, w_neigh2)


def exchange(x):
    return lax.all_to_all(x, "dom", split_axis=0, concat_axis=0, tiled=True)


def local(
    features, owner, slot, send_blocks, tile_row, tile_col, tile_vals, tile_count,
    w_self1, w_neigh1, w_self2, w_neigh2,
):
    picks = send_blocks.reshape(ND)
    features = pltpu.with_memory_space_constraint(features, pltpu.HBM)
    packed = pack(features, owner, slot).reshape(ND, SEG // 2, 2, F)
    arrived = pltpu.with_memory_space_constraint(exchange(packed).reshape(ND * SEG, F), pltpu.VMEM)
    relaid, send = unpack(picks, arrived)
    near = exchange(send)
    pairs, base, inv, lists = prepare(tile_row, tile_col, tile_count, picks, tile_vals, relaid)
    mean, send = first(lists, pairs, near, base, inv)
    far = exchange(send)
    base = own_part(lists, pairs, relaid, mean, inv, w_self1, w_neigh1, w_self2, w_neigh2)
    return second(lists, near, far, pairs, base, inv, w_self1, w_neigh1, w_neigh2).reshape(ROWS, H)


def solution(mesh):
    rows, flat = P("dom", None), P("dom")
    cube = P("dom", None, None)
    placed = (rows, flat, flat, cube, flat, flat, cube, flat, P(), P(), P(), P())
    return jax.shard_map(local, mesh=mesh, in_specs=placed, out_specs=rows, check_vma=False)
```

```python
import jax
import jax.numpy as jnp
from jax import lax
from jax.experimental import pallas as pl
from jax.experimental.pallas import tpu as pltpu
from jax.sharding import PartitionSpec as P

F = 128
H = 256
BLK = 128
ROWS = 4096
TILES = 256
NB = 32
ND = 128
PER = ROWS // ND
SEG = PER + 2
PAIRS = 192
GROUP = 16
BATCH = 8
BATCHES = NB // BATCH
UNROLL = 4
ROW, COL, META, DEST, DEST_AT, LISTS = 0, PAIRS, 3 * PAIRS, 3 * PAIRS + 8, 3 * PAIRS + 136, 1024
BF = jnp.bfloat16
F32 = jnp.float32
I32 = jnp.int32

SMEM = pl.BlockSpec(memory_space=pltpu.SMEM)
VMEM = pl.BlockSpec(memory_space=pltpu.VMEM)
ANY = pl.BlockSpec(memory_space=pl.ANY)


def params(mib):
    return pltpu.CompilerParams(vmem_limit_bytes=mib * 1024 * 1024)


def cost(flops, nbytes):
    return pl.CostEstimate(flops=flops, bytes_accessed=nbytes, transcendentals=0)


def mm(a, b):
    return jnp.dot(a, b, preferred_element_type=F32)


def mm_t(a, b):
    return lax.dot_general(a, b, (((1,), (1,)), ((), ())), preferred_element_type=F32)


POSTS = 16
PARTS = 4


def pack_kernel(owner_in, slot_in, feat, out, rows, held, owner, slot, pos_v, pos_s, sems, sem_feat, sem_owner, sem_slot):
    load_owner = pltpu.make_async_copy(owner_in, owner, sem_owner)
    load_slot = pltpu.make_async_copy(slot_in, slot, sem_slot)
    load = pltpu.make_async_copy(feat, held, sem_feat)
    load_owner.start()
    load_slot.start()
    load.start()
    sub = lax.broadcasted_iota(I32, (BLK, BLK), 0)
    lane = lax.broadcasted_iota(I32, (BLK, BLK), 1)
    before = jnp.concatenate([(sub < lane).astype(BF), jnp.ones((BLK, BLK), BF)], axis=1)
    carry = jnp.zeros((BLK, BLK), F32)
    digits = jnp.zeros((BLK, BLK), F32)
    load_owner.wait()
    load_slot.wait()
    step = ROWS // BLK // PARTS

    def to_scalar(q):
        part = pl.ds(q * step, step)
        return pltpu.make_async_copy(pos_v.at[part], pos_s.at[part], sems.at[q])

    for c in range(ROWS // BLK):
        own = owner[c : c + 1, :]
        hit = own == sub
        hit_f = hit.astype(F32)
        counts = mm(hit_f.astype(BF), before)
        rank = jnp.sum(hit_f * (counts[:, :BLK] + carry), axis=0, keepdims=True)
        carry = carry + counts[:, BLK:]
        rank_i = rank.astype(I32)
        pos_v[c : c + 1, :] = own * SEG + rank_i
        places = slot[c : c + 1, :]
        high = (places >> 6).astype(F32)
        low = (places & 63).astype(F32)
        spread = jnp.concatenate([hit_f * high, hit_f * low], axis=1).astype(BF)
        ranks = jnp.concatenate([rank_i == sub, rank_i + PER == sub], axis=1).astype(F32).astype(BF)
        digits = digits + mm_t(spread, ranks)
        if c % step == step - 1:
            to_scalar(c // step).start()
    for extra in range(PER, SEG):
        rows[pl.ds(extra, ND, stride=SEG), :] = digits
    load.wait()

    def move(c, _):
        for u in range(BLK):
            rows[pl.ds(pos_s[c, u], 1), :] = held[pl.ds(c * BLK + u, 1), :]
        return 0

    def moves(q, _):
        to_scalar(q).wait()
        return lax.fori_loop(q * step, (q + 1) * step, move, 0)

    lax.fori_loop(0, PARTS, moves, 0)
    out[...] = rows[...].astype(BF)


def pack(features, owner, slot):
    return pl.pallas_call(
        pack_kernel,
        out_shape=pltpu.VMEM((ND * SEG, F), BF),
        in_specs=[ANY] * 3,
        out_specs=VMEM,
        scratch_shapes=[
            pltpu.VMEM((ND * SEG, F), F32),
            pltpu.VMEM((ROWS, F), F32),
            pltpu.VMEM((ROWS // BLK, BLK), I32),
            pltpu.VMEM((ROWS // BLK, BLK), I32),
            pltpu.VMEM((ROWS // BLK, BLK), I32),
            pltpu.SMEM((ROWS // BLK, BLK), I32),
            pltpu.SemaphoreType.DMA((PARTS,)),
        ]
        + [pltpu.SemaphoreType.DMA] * 3,
        compiler_params=params(56),
        name="pack",
    )(owner.reshape(ROWS // BLK, BLK), slot.reshape(ROWS // BLK, BLK), features)


def unpack_kernel(
    send_in, arrived, relaid_out, send,
    send_blocks, rows, placed, relaid, slot_v, slot_s, sem_send, sems, sem_relaid, sem_out,
):
    load_send = pltpu.make_async_copy(send_in, send_blocks, sem_send)
    load_send.start()
    senders = ND // PARTS
    step = senders * PER // F
    lane = lax.broadcasted_iota(I32, (step, F), 1)

    def to_scalar(q):
        part = pl.ds(q * step, step)
        return pltpu.make_async_copy(slot_v.at[part], slot_s.at[part], sems.at[q])

    for q in range(PARTS):
        size = senders * SEG
        rows[pl.ds(q * size, size), :] = arrived[pl.ds(q * size, size), :].astype(F32)
        digits = rows[pl.ds(q * size + PER, senders, stride=SEG), :]
        slots = digits * 64.0 + pltpu.roll(digits, F - PER, 1)
        total = jnp.where(lane < PER, slots[:step], 0.0)
        for g in range(1, F // PER):
            total += pltpu.roll(jnp.where(lane < PER, slots[step * g : step * (g + 1)], 0.0), PER * g, 1)
        slot_v[pl.ds(q * step, step), :] = total.astype(I32)
        to_scalar(q).start()

    def moves(q, _):
        to_scalar(q).wait()

        def move(i, _):
            for u in range(F):
                source = (q * senders + i + step * (u // PER)) * SEG + u % PER
                placed[pl.ds(slot_s[q * step + i, u], 1), :] = rows[pl.ds(source, 1), :]
            return 0

        return lax.fori_loop(0, step, move, 0)

    lax.fori_loop(0, PARTS, moves, 0)
    relaid[...] = placed[...].reshape(NB, BLK, F).astype(BF)
    load_send.wait()

    def post(i, _):
        for u in range(POSTS):
            d = i * POSTS + u
            pltpu.make_async_copy(relaid.at[send_blocks[d]], send.at[d], sem_out).start()
        return 0

    lax.fori_loop(0, ND // POSTS, post, 0)
    keep = pltpu.make_async_copy(relaid, relaid_out, sem_relaid)
    keep.start()
    pltpu.make_async_copy(send, send, sem_out).wait()
    keep.wait()


def unpack(send_blocks, arrived):
    return pl.pallas_call(
        unpack_kernel,
        out_shape=(
            pltpu.HBM((NB, BLK, F), BF),
            pltpu.HBM((ND, BLK, F), BF),
        ),
        in_specs=[ANY, VMEM],
        out_specs=(ANY, ANY),
        scratch_shapes=[
            pltpu.SMEM((ND,), I32),
            pltpu.VMEM((ND * SEG, F), F32),
            pltpu.VMEM((ROWS, F), F32),
            pltpu.VMEM((NB, BLK, F), BF),
            pltpu.VMEM((PER, F), I32),
            pltpu.SMEM((PER, F), I32),
            pltpu.SemaphoreType.DMA,
            pltpu.SemaphoreType.DMA((PARTS,)),
            pltpu.SemaphoreType.DMA,
            pltpu.SemaphoreType.DMA,
        ],
        compiler_params=params(56),
        name="unpack",
    )(send_blocks, arrived)


def prepare_kernel(
    row_s, col_s, count_s, send_blocks, tile_vals, relaid,
    pairs, base, inv_out, lists,
    tiles, acc, held, cursor, tile_k, sem,
):
    load = pltpu.make_async_copy(tile_vals, tiles.at[pl.ds(0, TILES)], sem)
    load.start()
    tiles[TILES] = jnp.zeros((BLK, BLK), I32)
    acc[...] = jnp.zeros_like(acc)

    def clear(i, _):
        cursor[i] = 0
        return 0

    lax.fori_loop(0, 2 * NB, clear, 0)

    def clear_pair(i, _):
        lists[ROW + i] = 0
        for s in (0, 1):
            tile_k[2 * i + s] = TILES
            lists[COL + 2 * i + s] = 0
        return 0

    lax.fori_loop(0, PAIRS, clear_pair, 0)
    used = count_s[0]

    def tally(t, _):
        g = row_s[t] + jnp.where(col_s[t] >= NB, NB, 0)
        cursor[g] = cursor[g] + 1
        return 0

    lax.fori_loop(0, used, tally, 0)

    def starts(g, at):
        n = cursor[g]
        cursor[g] = 2 * at
        return at + ((n + 1) >> 1)

    n_own = lax.fori_loop(0, NB, starts, 0)
    n_own = (n_own + GROUP - 1) // GROUP * GROUP
    n_all = lax.fori_loop(NB, 2 * NB, starts, n_own)
    n_all = (n_all + GROUP - 1) // GROUP * GROUP
    lists[META + 0] = n_own
    lists[META + 1] = n_all

    def place(t, _):
        row = row_s[t]
        col = col_s[t]
        far = col >= NB
        col = jnp.where(far, col - NB, col)
        g = row + jnp.where(far, NB, 0)
        at = cursor[g]
        cursor[g] = at + 1
        tile_k[at] = t
        lists[COL + at] = col
        lists[ROW + at >> 1] = row
        return 0

    lax.fori_loop(0, used, place, 0)

    def zero_dest(i, _):
        cursor[i] = 0
        return 0

    lax.fori_loop(0, NB, zero_dest, 0)

    def tally_dest(d, _):
        b = send_blocks[d]
        cursor[b] = cursor[b] + 1
        return 0

    lax.fori_loop(0, ND, tally_dest, 0)

    def starts_dest(b, at):
        n = cursor[b]
        cursor[b] = at
        lists[DEST_AT + b] = at
        return at + n

    lists[DEST_AT + NB] = lax.fori_loop(0, NB, starts_dest, 0)

    def place_dest(d, _):
        b = send_blocks[d]
        at = cursor[b]
        cursor[b] = at + 1
        lists[DEST + at] = d
        return 0

    lax.fori_loop(0, ND, place_dest, 0)
    load.wait()
    ones = jnp.ones((2 * BLK, BLK), BF)

    def fetch(k):
        v = jnp.concatenate([tiles[tile_k[2 * k]], tiles[tile_k[2 * k + 1]]], axis=1)
        v = v.astype(F32).astype(BF)
        pairs[k] = v
        return v

    def own(i, _):
        for u in range(UNROLL):
            k = i * UNROLL + u
            v = fetch(k)
            x = jnp.concatenate([relaid[lists[COL + 2 * k]], relaid[lists[COL + 2 * k + 1]]], axis=0)
            got = mm(v, jnp.concatenate([x, ones], axis=1))
            acc[lists[ROW + k]] += got
        return 0

    lax.fori_loop(0, n_own // UNROLL, own, 0)

    def far(i, _):
        for u in range(UNROLL):
            k = i * UNROLL + u
            r = lists[ROW + k]
            acc[r, :, BLK:] += mm(fetch(k), ones)
        return 0

    lax.fori_loop(n_own // UNROLL, n_all // UNROLL, far, 0)
    inv = 1.0 / jnp.maximum(acc[:, :, BLK:], 1.0)
    inv_out[...] = inv
    base[...] = acc[:, :, :BLK] * inv


def prepare(tile_row, tile_col, tile_count, send_blocks, tile_vals, relaid):
    return pl.pallas_call(
        prepare_kernel,
        out_shape=(
            jax.ShapeDtypeStruct((PAIRS, BLK, 2 * BLK), BF),
            jax.ShapeDtypeStruct((NB, BLK, F), F32),
            jax.ShapeDtypeStruct((NB, BLK, BLK), F32),
            jax.ShapeDtypeStruct((LISTS,), I32),
        ),
        in_specs=[SMEM, SMEM, SMEM, SMEM, ANY, VMEM],
        out_specs=(VMEM, VMEM, VMEM, SMEM),
        scratch_shapes=[
            pltpu.VMEM((TILES + 1, BLK, BLK), I32),
            pltpu.VMEM((NB, BLK, 2 * BLK), F32),
            pltpu.VMEM((8, BLK), F32),
            pltpu.SMEM((2 * NB,), I32),
            pltpu.SMEM((2 * PAIRS,), I32),
            pltpu.SemaphoreType.DMA,
        ],
        compiler_params=params(56),
        cost_estimate=cost(2 * 10**9, 32 * 2**20),
        name="prepare",
    )(tile_row, tile_col, tile_count, send_blocks, tile_vals, relaid)


def load_pairs(first, last, pairs, held, sems, begin=0, end=PAIRS):
    def group(c, _):
        pltpu.make_async_copy(
            pairs.at[pl.ds(first + c * GROUP, GROUP)], held.at[pl.ds(c * GROUP, GROUP)], sems.at[c]
        ).start()
        return 0

    groups = (last - first) // GROUP
    lax.fori_loop(jnp.minimum(begin, groups), jnp.minimum(end, groups), group, 0)


def row_copies(i, base, inv, base_v, inv_v, sems_base, sems_inv):
    b = pl.ds(BATCH * i, BATCH)
    return (
        pltpu.make_async_copy(base.at[b], base_v.at[b], sems_base.at[i]),
        pltpu.make_async_copy(inv.at[b], inv_v.at[b], sems_inv.at[i]),
    )


def add_pairs(first, last, held, sems, table, acc, lists, finish):
    groups = (last - first) // GROUP

    def group(c, done):
        pltpu.make_async_copy(held.at[pl.ds(0, GROUP)], held.at[pl.ds(0, GROUP)], sems.at[c]).wait()
        for u0 in range(0, GROUP, UNROLL):
            for u in range(u0, u0 + UNROLL):
                k = first + c * GROUP + u
                x = jnp.concatenate([table[lists[COL + 2 * k]], table[lists[COL + 2 * k + 1]]], axis=0)
                got = mm(held[c * GROUP + u], x)
                acc[lists[ROW + k]] += got
        following = lists[ROW + jnp.minimum(first + (c + 1) * GROUP, PAIRS - 1)]
        upto = jnp.where(c + 1 < groups, following, NB) // BATCH
        lax.fori_loop(done, upto, finish, 0)
        return upto

    lax.fori_loop(lax.fori_loop(0, groups, group, 0), BATCHES, finish, 0)


def first_kernel(
    lists_in, remote, pairs, base, inv, mean_out, send,
    lists, table, held, base_v, inv_v, acc, mean, sems, sems_base, sems_inv, sem_lists, sem_table, sem_mean, sem_out,
):
    load_table = pltpu.make_async_copy(remote, table, sem_table)
    rows = lambda i: row_copies(i, base, inv, base_v, inv_v, sems_base, sems_inv)

    def load(i, _):
        load_pairs(lists[META + 0], lists[META + 1], pairs, held, sems, LOADS * i, LOADS * (i + 1))
        for copy in rows(i):
            copy.start()
        return 0

    load_lists = pltpu.make_async_copy(lists_in, lists, sem_lists)
    load_lists.start()
    load_table.start()
    load_lists.wait()
    lax.fori_loop(0, EARLY, load, 0)
    acc[...] = jnp.zeros_like(acc)
    load_table.wait()
    lax.fori_loop(EARLY, BATCHES, load, 0)
    load_pairs(lists[META + 0], lists[META + 1], pairs, held, sems, LOADS * BATCHES)

    def finish(i, _):
        for copy in rows(i):
            copy.wait()
        b = pl.ds(BATCH * i, BATCH)
        mean[b] = (base_v[b] + acc[b] * inv_v[b]).astype(BF)
        pltpu.make_async_copy(mean.at[b], mean_out.at[b], sem_mean).start()

        def post(j, blk):
            blk = lax.while_loop(lambda at: j >= lists[DEST_AT + at + 1], lambda at: at + 1, blk)
            pltpu.make_async_copy(mean.at[blk], send.at[lists[DEST + j]], sem_out).start()
            return blk

        lax.fori_loop(lists[DEST_AT + BATCH * i], lists[DEST_AT + BATCH * (i + 1)], post, BATCH * i)
        return 0

    add_pairs(lists[META + 0], lists[META + 1], held, sems, table, acc, lists, finish)
    pltpu.make_async_copy(mean_out, mean_out, sem_mean).wait()
    pltpu.make_async_copy(send, send, sem_out).wait()


def first(lists, pairs, remote, base, inv):
    return pl.pallas_call(
        first_kernel,
        out_shape=(
            jax.ShapeDtypeStruct((NB, BLK, F), BF),
            jax.ShapeDtypeStruct((ND, BLK, F), BF),
        ),
        in_specs=[ANY] * 5,
        out_specs=(ANY, ANY),
        scratch_shapes=[
            pltpu.SMEM((LISTS,), I32),
            pltpu.VMEM((ND, BLK, F), BF),
            pltpu.VMEM((PAIRS, BLK, 2 * BLK), BF),
            pltpu.VMEM((NB, BLK, F), F32),
            pltpu.VMEM((NB, BLK, BLK), F32),
            pltpu.VMEM((NB, BLK, F), F32),
            pltpu.VMEM((NB, BLK, F), BF),
            pltpu.SemaphoreType.DMA((PAIRS // GROUP,)),
            pltpu.SemaphoreType.DMA((BATCHES,)),
            pltpu.SemaphoreType.DMA((BATCHES,)),
        ]
        + [pltpu.SemaphoreType.DMA] * 4,
        compiler_params=params(56),
        name="first_layer",
    )(lists, remote, pairs, base, inv)


def own_kernel(
    lists, pairs, relaid, mean, inv, w_self1, w_neigh1, w_self2, w_neigh2, base,
    hidden, acc, held, sems,
):
    load_pairs(0, lists[META + 0], pairs, held, sems)
    acc[...] = jnp.zeros_like(acc)
    weights = jnp.concatenate([w_self1[...], w_neigh1[...]], axis=0)
    final = jnp.concatenate([w_self2[...], w_neigh2[...], w_neigh2[...]], axis=0)

    def layer(i, _):
        b = pl.ds(2 * i, 2)
        x = jnp.concatenate([relaid[b].reshape(2 * BLK, F), mean[b].reshape(2 * BLK, F)], axis=1)
        hidden[b] = jnp.maximum(mm(x, weights), 0.0).astype(BF).reshape(2, BLK, H)
        return 0

    lax.fori_loop(0, NB // 2, layer, 0)

    def finish(i, _):
        b = pl.ds(BATCH * i, BATCH)
        scale = inv[b].reshape(BATCH * BLK, BLK)
        m = acc[b].reshape(BATCH * BLK, H) * jnp.concatenate([scale, scale], axis=1)
        high = m.astype(BF)
        low = (m - high.astype(F32)).astype(BF)
        x = jnp.concatenate([hidden[b].reshape(BATCH * BLK, H), high, low], axis=1)
        base[b] = mm(x, final).reshape(BATCH, BLK, H)
        return 0

    add_pairs(0, lists[META + 0], held, sems, hidden, acc, lists, finish)


def own_part(lists, pairs, relaid, mean, inv, w_self1, w_neigh1, w_self2, w_neigh2):
    return pl.pallas_call(
        own_kernel,
        out_shape=jax.ShapeDtypeStruct((NB, BLK, H), F32),
        in_specs=[SMEM, ANY] + [VMEM] * 7,
        out_specs=VMEM,
        scratch_shapes=[
            pltpu.VMEM((NB, BLK, H), BF),
            pltpu.VMEM((NB, BLK, H), F32),
            pltpu.VMEM((PAIRS, BLK, 2 * BLK), BF),
            pltpu.SemaphoreType.DMA((PAIRS // GROUP,)),
        ],
        compiler_params=params(56),
        cost_estimate=cost(2 * 10**9, 32 * 2**20),
        name="own_part",
    )(lists, pairs, relaid, mean, inv, w_self1, w_neigh1, w_self2, w_neigh2)


EARLY = 2
LOADS = 2
CHUNK = ND // BATCHES


def second_kernel(
    lists, near, far, pairs, base, inv, w_self1, w_neigh1, w_neigh2, out,
    near_v, far_v, table, held, base_v, inv_v, acc, result,
    sems, sems_near, sems_far, sems_base, sems_inv, sem_out,
):
    def chunk(c):
        part = pl.ds(c * CHUNK, CHUNK)
        return (
            pltpu.make_async_copy(near.at[part], near_v.at[part], sems_near.at[c]),
            pltpu.make_async_copy(far.at[part], far_v.at[part], sems_far.at[c]),
        )

    rows = lambda i: row_copies(i, base, inv, base_v, inv_v, sems_base, sems_inv)

    def load(i):
        load_pairs(lists[META + 0], lists[META + 1], pairs, held, sems, LOADS * i, LOADS * (i + 1))
        for copy in rows(i):
            copy.start()

    for c in range(ND // CHUNK):
        for copy in chunk(c):
            copy.start()
    acc[...] = jnp.zeros_like(acc)
    weights = jnp.concatenate([w_self1[...], w_neigh1[...]], axis=0)

    def layer(c, _):
        for copy in chunk(c):
            copy.wait()
        load(c)
        for i in range(CHUNK // 2):
            b = pl.ds(c * CHUNK + 2 * i, 2)
            x = jnp.concatenate([near_v[b].reshape(2 * BLK, F), far_v[b].reshape(2 * BLK, F)], axis=1)
            table[b] = jnp.maximum(mm(x, weights), 0.0).astype(BF).reshape(2, BLK, H)
        return 0

    lax.fori_loop(0, BATCHES, layer, 0)
    load_pairs(lists[META + 0], lists[META + 1], pairs, held, sems, LOADS * BATCHES)

    def finish(i, _):
        for copy in rows(i):
            copy.wait()
        b = pl.ds(BATCH * i, BATCH)
        scale = inv_v[b].reshape(BATCH * BLK, BLK)
        m = acc[b].reshape(BATCH * BLK, H) * jnp.concatenate([scale, scale], axis=1)
        total = base_v[b].reshape(BATCH * BLK, H) + mm(m.astype(BF), w_neigh2[...])
        result[b] = total.astype(BF).reshape(BATCH, BLK, H)
        pltpu.make_async_copy(result.at[b], out.at[b], sem_out).start()
        return 0

    add_pairs(lists[META + 0], lists[META + 1], held, sems, table, acc, lists, finish)
    pltpu.make_async_copy(out, out, sem_out).wait()


def second(lists, near, far, pairs, base, inv, w_self1, w_neigh1, w_neigh2):
    return pl.pallas_call(
        second_kernel,
        out_shape=jax.ShapeDtypeStruct((NB, BLK, H), BF),
        in_specs=[SMEM] + [ANY] * 5 + [VMEM] * 3,
        out_specs=ANY,
        scratch_shapes=[
            pltpu.VMEM((ND, BLK, F), BF),
            pltpu.VMEM((ND, BLK, F), BF),
            pltpu.VMEM((ND, BLK, H), BF),
            pltpu.VMEM((PAIRS, BLK, 2 * BLK), BF),
            pltpu.VMEM((NB, BLK, H), F32),
            pltpu.VMEM((NB, BLK, BLK), F32),
            pltpu.VMEM((NB, BLK, H), F32),
            pltpu.VMEM((NB, BLK, H), BF),
            pltpu.SemaphoreType.DMA((PAIRS // GROUP,)),
        ]
        + [pltpu.SemaphoreType.DMA((BATCHES,))] * 4
        + [pltpu.SemaphoreType.DMA],
        compiler_params=params(56),
        name="second_layer",
    )(lists, near, far, pairs, base, inv, w_self1, w_neigh1, w_neigh2)


def exchange(x):
    return lax.all_to_all(x, "dom", split_axis=0, concat_axis=0, tiled=True)


def local(
    features, owner, slot, send_blocks, tile_row, tile_col, tile_vals, tile_count,
    w_self1, w_neigh1, w_self2, w_neigh2,
):
    picks = send_blocks.reshape(ND)
    features = pltpu.with_memory_space_constraint(features, pltpu.HBM)
    packed = pack(features, owner, slot).reshape(ND, SEG // 2, 2, F)
    arrived = pltpu.with_memory_space_constraint(exchange(packed).reshape(ND * SEG, F), pltpu.VMEM)
    relaid, send = unpack(picks, arrived)
    near = exchange(send)
    pairs, base, inv, lists = prepare(tile_row, tile_col, tile_count, picks, tile_vals, relaid)
    mean, send = first(lists, pairs, near, base, inv)
    far = exchange(send)
    base = own_part(lists, pairs, relaid, mean, inv, w_self1, w_neigh1, w_self2, w_neigh2)
    return second(lists, near, far, pairs, base, inv, w_self1, w_neigh1, w_neigh2).reshape(ROWS, H)


def solution(mesh):
    rows, flat = P("dom", None), P("dom")
    cube = P("dom", None, None)
    placed = (rows, flat, flat, cube, flat, flat, cube, flat, P(), P(), P(), P())
    return jax.shard_map(local, mesh=mesh, in_specs=placed, out_specs=rows, check_vma=False)
```
